256 devices in a mesh: dp: 4 (over y), point: 64 (over z, x, core).
Axes of the slice: x: 4, y: 4, z: 8, core: 2. Of those that a mesh axis runs over, the one named last changes fastest.
Arguments:
- mesh_element_data: bfloat16 [4, 49152, 256], P('dp', 'point'), may hold values from -6 to 6
- loss_sensitivity: bfloat16 [4, 49152, 256], P('dp', 'point'), may hold values from -0.75 to 0.75
- leading_scale_factor: float32 [256], replicated, may hold values from 0.1 to 1.9
- intermediate_map_matrix: bfloat16 [256, 256], replicated, may hold values from -0.375 to 0.375
- partitioned_map_matrix: bfloat16 [256, 256], replicated, may hold values from -0.375 to 0.375
- partition_score_matrix: bfloat16 [32, 64], replicated, may hold values from -1 to 1
- softening_factor: float32 [8], replicated, may hold values from 0.3 to 1
- asking_matrix: bfloat16 [32, 32], replicated, may hold values from -1 to 1
- lookup_matrix: bfloat16 [32, 32], replicated, may hold values from -1 to 1
- content_matrix: bfloat16 [32, 32], replicated, may hold values from -1 to 1
- result_matrix: bfloat16 [256, 256], replicated, may hold values from -0.375 to 0.375
- trailing_scale_factor: float32 [256], replicated, may hold values from 0.1 to 1.9
- expanding_matrix: bfloat16 [256, 1024], replicated, may hold values from -0.375 to 0.375
- contracting_matrix: bfloat16 [1024, 256], replicated, may hold values from -0.1875 to 0.1875
Outputs:
- grad_cells: bfloat16 [4, 49152, 256], P('dp', 'point')
- grad_gain_first: float32 [256], replicated
- grad_proj_mid: float32 [256, 256], replicated
- grad_proj_feat: float32 [256, 256], replicated
- grad_proj_slice: float32 [32, 64], replicated
- grad_temperature: float32 [8], replicated
- grad_w_query: float32 [32, 32], replicated
- grad_w_key: float32 [32, 32], replicated
- grad_w_value: float32 [32, 32], replicated
- grad_w_out: float32 [256, 256], replicated
- grad_gain_second: float32 [256], replicated
- grad_w_up: float32 [256, 1024], replicated
- grad_w_down: float32 [1024, 256], replicated
The draws below stay inside these ranges and needn't reach their ends.
All inputs are finite; a program needn't handle non-finite values.
Results may differ from the reference program's by a relative error of at most 0.024.
Values sent between devices are 32-bit elements; how exact they have to be, the bound alone decides.
A program may use at most 64 MiB of HBM per device.

```python
import math
import jax
import jax.numpy as jnp
from jax import lax

D = 256
HEAD_COUNT = 8
SLICES = 64
FF = 1024
CELLS_DEV = 768
HEAD_DIM = 32
CELLS = 49152
SAMPLES = 4
N_POINT = 64


def block_levels(rng, shape, cuts, least, top_value):
    loudness = 1.0
    for position, blocks in cuts:
        draws = jax.random.uniform(jax.random.fold_in(jax.random.fold_in(rng, 6), position), (blocks,), jnp.float32, least / len(cuts), top_value / len(cuts))
        loudness = loudness * jnp.repeat(jnp.exp(draws), shape[position] // blocks).reshape((-1,) + (1,) * (len(shape) - 1 - position))
    return loudness


def noise(key, dims, scale, most, cuts=(), kind=jnp.bfloat16):
    level = block_levels(key, dims, cuts, -0.22, 0.18) if cuts else 1.0
    array = jax.random.normal(key, dims, jnp.float32) * scale * level
    return jnp.minimum(jnp.maximum(array, -most), most).astype(kind)


def setup_inputs(seed: int = 0) -> dict:
    keys = jax.random.split(jax.random.key(seed), 15)
    mesh_element_data = noise(keys[0], (SAMPLES, CELLS, D), 1.0, 6.0, ((0, 4), (1, 64)))
    loss_sensitivity = noise(keys[1], (SAMPLES, CELLS, D), ((CELLS * SAMPLES) ** -0.25), 0.75, ((0, 4), (1, 64)))
    leading_scale_factor = jnp.clip(1.0 + 0.18 * jax.random.normal(keys[2], (D,), jnp.float32), 0.1, 1.9)
    intermediate_map_matrix = noise(keys[3], (D, D), D ** -0.5, 0.375)
    partitioned_map_matrix = noise(keys[4], (D, D), D ** -0.5, 0.375)
    partition_score_matrix = noise(keys[5], (HEAD_DIM, SLICES), HEAD_DIM ** -0.5, 1.0)
    softening_factor = jnp.clip(jnp.exp(jax.random.uniform(keys[6], (HEAD_COUNT,), jnp.float32, math.log(0.3), math.log(1.0))), 0.3, 1.0)
    asking_matrix = noise(keys[7], (HEAD_DIM, HEAD_DIM), HEAD_DIM ** -0.5, 1.0)
    lookup_matrix = noise(keys[8], (HEAD_DIM, HEAD_DIM), HEAD_DIM ** -0.5, 1.0)
    content_matrix = noise(keys[9], (HEAD_DIM, HEAD_DIM), HEAD_DIM ** -0.5, 1.0)
    result_matrix = noise(keys[10], (D, D), D ** -0.5, 0.375)
    trailing_scale_factor = jnp.clip(1.0 + 0.18 * jax.random.normal(keys[11], (D,), jnp.float32), 0.1, 1.9)
    expanding_matrix = noise(keys[12], (D, FF), D ** -0.5, 0.375)
    contracting_matrix = noise(keys[13], (FF, D), FF ** -0.5, 0.1875)
    return dict(mesh_element_data=mesh_element_data, loss_sensitivity=loss_sensitivity, leading_scale_factor=leading_scale_factor, intermediate_map_matrix=intermediate_map_matrix, partitioned_map_matrix=partitioned_map_matrix, partition_score_matrix=partition_score_matrix, softening_factor=softening_factor, asking_matrix=asking_matrix, lookup_matrix=lookup_matrix, content_matrix=content_matrix, result_matrix=result_matrix, trailing_scale_factor=trailing_scale_factor, expanding_matrix=expanding_matrix, contracting_matrix=contracting_matrix)


def norm_rows(values, gain):
    centre = lax.optimization_barrier(jnp.mean(values, axis=1, keepdims=True))
    centred = values - centre
    spread = lax.optimization_barrier(jnp.mean(centred * centred, axis=1, keepdims=True))
    return (centred * lax.rsqrt(spread + 1e-05) * gain).astype(jnp.bfloat16)

def partition_share(incoming_entries, leading_scale_factor, intermediate_map_matrix, partitioned_map_matrix, partition_score_matrix, softening_factor):
    count = incoming_entries.shape[0]
    normed = norm_rows(incoming_entries, leading_scale_factor)
    middle = jnp.dot(normed, intermediate_map_matrix, preferred_element_type=jnp.float32).reshape(count, HEAD_COUNT, HEAD_DIM)
    feature = jnp.dot(normed, partitioned_map_matrix, preferred_element_type=jnp.float32).reshape(count, HEAD_COUNT, HEAD_DIM)
    partition_scores = jnp.einsum('che,em->chm', middle, partition_score_matrix.astype(jnp.float32), precision=lax.Precision.HIGHEST)
    exponentiated_scores = jnp.exp(partition_scores / softening_factor[None, :, None])
    partition_probabilities = exponentiated_scores / lax.optimization_barrier(jnp.sum(exponentiated_scores, axis=2, keepdims=True))
    aggregated_states = jnp.einsum('chm,che->hme', partition_probabilities, feature, precision=lax.Precision.HIGHEST)
    partition_mass = lax.optimization_barrier(jnp.sum(partition_probabilities, axis=0))
    return (aggregated_states, partition_mass, partition_probabilities.reshape(count, HEAD_COUNT * SLICES))

def token_mix(aggregated_states, partition_mass, asking_matrix, lookup_matrix, content_matrix):
    tokens = aggregated_states / partition_mass[:, :, None]
    queries = jnp.einsum('hme,ef->hmf', tokens, asking_matrix.astype(jnp.float32), precision=lax.Precision.HIGHEST)
    key_rows = jnp.einsum('hme,ef->hmf', tokens, lookup_matrix.astype(jnp.float32), precision=lax.Precision.HIGHEST)
    value_rows = jnp.einsum('hme,ef->hmf', tokens, content_matrix.astype(jnp.float32), precision=lax.Precision.HIGHEST)
    scores = jnp.einsum('hmf,hnf->hmn', queries, key_rows, precision=lax.Precision.HIGHEST) * HEAD_DIM ** (-0.5)
    exponentiated_scores = jnp.exp(scores)
    probs = exponentiated_scores / lax.optimization_barrier(jnp.sum(exponentiated_scores, axis=2, keepdims=True))
    return jnp.einsum('hmn,hnf->hmf', probs, value_rows, precision=lax.Precision.HIGHEST)

def mix_part(incoming_entries, partition_probabilities, mixed_tokens, result_matrix, trailing_scale_factor, expanding_matrix, contracting_matrix):
    count = incoming_entries.shape[0]
    spread = jnp.einsum('chm,hme->che', partition_probabilities.reshape(count, HEAD_COUNT, SLICES), mixed_tokens, precision=lax.Precision.HIGHEST).reshape(count, D).astype(jnp.bfloat16)
    state = incoming_entries + jnp.dot(spread, result_matrix, preferred_element_type=jnp.float32)
    normed = norm_rows(state, trailing_scale_factor)
    hidden = jax.nn.gelu(jnp.dot(normed, expanding_matrix, preferred_element_type=jnp.float32), approximate=True).astype(jnp.bfloat16)
    return state + jnp.dot(hidden, contracting_matrix, preferred_element_type=jnp.float32)

def as_float(values):
    return tuple((item.astype(jnp.float32) for item in values))

def lone_example_data(lone_element_entries, lone_sensitivity, leading_scale_factor, intermediate_map_matrix, partitioned_map_matrix, partition_score_matrix, softening_factor, asking_matrix, lookup_matrix, content_matrix, result_matrix, trailing_scale_factor, expanding_matrix, contracting_matrix):
    blocks_x = lone_element_entries.reshape(N_POINT, CELLS_DEV, D).astype(jnp.float32)
    blocks_dy = lone_sensitivity.reshape(N_POINT, CELLS_DEV, D).astype(jnp.float32)

    def forward_step(carry, incoming_entries):
        aggregated_states, partition_mass, ignored_scalar = partition_share(incoming_entries, leading_scale_factor, intermediate_map_matrix, partitioned_map_matrix, partition_score_matrix, softening_factor)
        return ((carry[0] + aggregated_states, carry[1] + partition_mass), None)
    start = (jnp.zeros((HEAD_COUNT, SLICES, HEAD_DIM), jnp.float32), jnp.zeros((HEAD_COUNT, SLICES), jnp.float32))
    (aggregated_states, partition_mass), ignored_scalar = lax.scan(forward_step, start, blocks_x)
    mixed_tokens, back_mix = jax.vjp(token_mix, aggregated_states, partition_mass, asking_matrix, lookup_matrix, content_matrix)

    def second_step(carry, pair):
        incoming_entries, dyrows = pair
        ignored_matrix, ignored_state_entry, partition_probabilities = partition_share(incoming_entries, leading_scale_factor, intermediate_map_matrix, partitioned_map_matrix, partition_score_matrix, softening_factor)
        unused_y, back_two = jax.vjp(mix_part, incoming_entries, partition_probabilities, mixed_tokens, result_matrix, trailing_scale_factor, expanding_matrix, contracting_matrix)
        dx_two, d_weights, d_tokens, g_out, g_gain, g_up, g_down = back_two(dyrows)
        derivative_collection = as_float((d_tokens, g_out, g_gain, g_up, g_down))
        carry = tuple((left + right for left, right in zip(carry, derivative_collection)))
        return (carry, (dx_two, d_weights))
    zeros_two = (jnp.zeros((HEAD_COUNT, SLICES, HEAD_DIM), jnp.float32), jnp.zeros((D, D), jnp.float32), jnp.zeros((D,), jnp.float32), jnp.zeros((D, FF), jnp.float32), jnp.zeros((FF, D), jnp.float32))
    sums_two, (dx_twos, d_weights_all) = lax.scan(second_step, zeros_two, (blocks_x, blocks_dy))
    d_weighted, d_totals, g_query, g_key, g_value = back_mix(sums_two[0])

    def first_step(carry, triple):
        incoming_entries, dx_two, d_weights = triple
        ignored_scalar, reverse_opening_pass = jax.vjp(partition_share, incoming_entries, leading_scale_factor, intermediate_map_matrix, partitioned_map_matrix, partition_score_matrix, softening_factor)
        dx_one, g_gain, g_mid, g_feat, g_slice, g_temp = reverse_opening_pass((d_weighted, d_totals, d_weights))
        derivative_collection = as_float((g_gain, g_mid, g_feat, g_slice, g_temp))
        carry = tuple((left + right for left, right in zip(carry, derivative_collection)))
        return (carry, (dx_one + dx_two).astype(jnp.bfloat16))
    zeros_one = (jnp.zeros((D,), jnp.float32), jnp.zeros((D, D), jnp.float32), jnp.zeros((D, D), jnp.float32), jnp.zeros((HEAD_DIM, SLICES), jnp.float32), jnp.zeros((HEAD_COUNT,), jnp.float32))
    sums_one, derivative_entry_series = lax.scan(first_step, zeros_one, (blocks_x, dx_twos, d_weights_all))
    mix_grads = as_float((g_query, g_key, g_value))
    derivative_collection = sums_one + mix_grads + sums_two[1:]
    return (derivative_entry_series.reshape(CELLS, D), derivative_collection)

def reference(mesh_element_data, loss_sensitivity, leading_scale_factor, intermediate_map_matrix, partitioned_map_matrix, partition_score_matrix, softening_factor, asking_matrix, lookup_matrix, content_matrix, result_matrix, trailing_scale_factor, expanding_matrix, contracting_matrix):
    grad_list = []
    partition_mass = None
    for example_data in range(SAMPLES):
        derivative_entry_series, derivative_collection = lone_example_data(mesh_element_data[example_data], loss_sensitivity[example_data], leading_scale_factor, intermediate_map_matrix, partitioned_map_matrix, partition_score_matrix, softening_factor, asking_matrix, lookup_matrix, content_matrix, result_matrix, trailing_scale_factor, expanding_matrix, contracting_matrix)
        grad_list.append(derivative_entry_series)
        partition_mass = derivative_collection if partition_mass is None else tuple((left + right for left, right in zip(partition_mass, derivative_collection)))
    grad_cells = jnp.stack(grad_list, axis=0)
    return (grad_cells, partition_mass[0], partition_mass[1], partition_mass[2], partition_mass[3], partition_mass[4], partition_mass[5], partition_mass[6], partition_mass[7], partition_mass[8], partition_mass[9], partition_mass[10], partition_mass[11])
```

```python
import functools
import jax
import jax.numpy as jnp
from jax import lax
from jax.experimental import pallas as pl
from jax.experimental.pallas import tpu as pltpu
from jax.sharding import PartitionSpec as P

MESH = pl.DeviceIdType.MESH
f32 = jnp.float32


def rcopy(src, dst, ss, rs, dev):
    return pltpu.make_async_remote_copy(
        src_ref=src, dst_ref=dst, send_sem=ss, recv_sem=rs, device_id=dev, device_id_type=MESH
    )


def where_am_i():
    y = lax.axis_index("dp")
    p = lax.axis_index("point")
    z = p // 8
    g = lax.rem(p, 8)
    x = g // 2
    c = lax.rem(g, 2)
    return y, z, x, c, g


def barrier(peers):
    sem = pltpu.get_barrier_semaphore()
    for dev in peers:
        pl.semaphore_signal(sem, inc=1, device_id=dev, device_id_type=MESH)
    pl.semaphore_wait(sem, len(peers))


def group_peers(z, g):
    return [{"point": z * 8 + lax.rem(g + d, 8)} for d in range(1, 8)]


def z_peers(z, g):
    return [{"point": lax.rem(z + d, 8) * 8 + g} for d in range(1, 8)]


def x_peers(z, x, c):
    return [{"point": z * 8 + lax.rem(x + d, 4) * 2 + c} for d in range(1, 4)]


def y_peers(y):
    return [{"dp": lax.rem(y + d, 4)} for d in range(1, 4)]


def small_kernel(s_ref, o_ref, rx1, rx2, ss, rs):
    y, z, x, c, g = where_am_i()
    gp, zp = group_peers(z, g), z_peers(z, g)
    barrier(gp + zp)
    cps = []
    for d in range(1, 8):
        cp = rcopy(s_ref.at[lax.rem(g + d, 8)], rx1.at[d - 1], ss.at[0, d - 1], rs.at[0, d - 1], gp[d - 1])
        cp.start()
        cps.append(cp)
    for cp in cps:
        cp.wait()
    acc = s_ref[g]
    for d in range(7):
        acc = acc + rx1[d]
    rx2[z] = acc
    cps = []
    for d in range(1, 8):
        cp = rcopy(rx2.at[z], rx2.at[z], ss.at[1, d - 1], rs.at[1, d - 1], zp[d - 1])
        cp.start()
        cps.append(cp)
    for cp in cps:
        cp.wait()
    acc = rx2[0]
    for d in range(1, 8):
        acc = acc + rx2[d]
    o_ref[g] = acc
    cps = []
    for d in range(1, 8):
        cp = rcopy(o_ref.at[g], o_ref.at[g], ss.at[2, d - 1], rs.at[2, d - 1], gp[d - 1])
        cp.start()
        cps.append(cp)
    for cp in cps:
        cp.wait()


def small_ar(v, cid):
    r = v.shape[1]
    return pl.pallas_call(
        small_kernel,
        out_shape=jax.ShapeDtypeStruct((8, r, 128), f32),
        in_specs=[pl.BlockSpec(memory_space=pltpu.VMEM)],
        out_specs=pl.BlockSpec(memory_space=pltpu.VMEM),
        scratch_shapes=[
            pltpu.VMEM((7, r, 128), f32),
            pltpu.VMEM((8, r, 128), f32),
            pltpu.SemaphoreType.DMA((3, 7)),
            pltpu.SemaphoreType.DMA((3, 7)),
        ],
        compiler_params=pltpu.CompilerParams(collective_id=cid, has_side_effects=True),
    )(v)


def add_into(dst, doff, rows, srcs, sl=None):
    t = min(rows, 64)

    def body(i, _):
        o = pl.multiple_of(i * t, t)
        acc = dst[pl.ds(doff + o, t), :]
        for s in srcs:
            acc = acc + s[pl.ds(o, t), :]
        dst[pl.ds(doff + o, t), :] = acc
        return 0

    lax.fori_loop(0, rows // t, body, 0)


def big_kernel(n, g_in, o_ref, gref, rx0, rx1, rx2, rx3, zb, zo, ss, rs):
    y, z, x, c, g = where_am_i()
    H, Q, E, F = n // 2, n // 4, n // 16, n // 64
    K = F // 2
    core = {"point": z * 8 + x * 2 + (1 - c)}
    xp, yp, zp = x_peers(z, x, c), y_peers(y), z_peers(z, g)
    barrier([core] + xp + yp + zp)
    m8 = lambda v: pl.multiple_of(v, 8)
    cp = rcopy(g_in.at[pl.ds(m8((1 - c) * H), H)], rx0, ss.at[0], rs.at[0], core)
    cp.start()

    def cpy(i, _):
        o = pl.multiple_of(i * 64, 64)
        gref[pl.ds(o, 64), :] = g_in[pl.ds(m8(c * H) + o, 64), :]
        return 0

    lax.fori_loop(0, H // 64, cpy, 0)
    cp.wait()
    add_into(gref, 0, H, [rx0])
    cps = []
    for d in range(1, 4):
        xi, yi = lax.rem(x + d, 4), lax.rem(y + d, 4)
        cps.append(rcopy(gref.at[pl.ds(m8(xi * E), E)], rx1.at[0, d - 1], ss.at[d], rs.at[d], xp[d - 1]))
        cps.append(rcopy(gref.at[pl.ds(m8(Q + yi * E), E)], rx1.at[1, d - 1], ss.at[3 + d], rs.at[3 + d], yp[d - 1]))
    for cp in cps:
        cp.start()
    for cp in cps:
        cp.wait()
    a0, b0 = m8(x * E), m8(Q + y * E)
    add_into(gref, a0, E, [rx1.at[0, d] for d in range(3)])
    add_into(gref, b0, E, [rx1.at[1, d] for d in range(3)])
    cps = []
    for d in range(1, 4):
        xi, yi = lax.rem(x + d, 4), lax.rem(y + d, 4)
        cps.append(rcopy(gref.at[pl.ds(m8(a0 + yi * F), F)], rx2.at[0, d - 1], ss.at[6 + d], rs.at[6 + d], yp[d - 1]))
        cps.append(rcopy(gref.at[pl.ds(m8(b0 + xi * F), F)], rx2.at[1, d - 1], ss.at[9 + d], rs.at[9 + d], xp[d - 1]))
    for cp in cps:
        cp.start()
    for cp in cps:
        cp.wait()
    a1, b1 = m8(a0 + y * F), m8(b0 + x * F)
    acc = gref[pl.ds(a1, F), :]
    for d in range(3):
        acc = acc + rx2[0, d]
    zb[0:F, :] = acc
    acc = gref[pl.ds(b1, F), :]
    for d in range(3):
        acc = acc + rx2[1, d]
    zb[F : 2 * F, :] = acc
    def zat(ref, k):
        return ref.at[pl.ds(m8((k // 2) * K), K), pl.ds(pl.multiple_of(lax.rem(k, 2) * 128, 128), 128)]

    cps = []
    for d in range(1, 8):
        zi = lax.rem(z + d, 8)
        cps.append(rcopy(zat(zb, zi), rx3.at[d - 1], ss.at[12 + d], rs.at[12 + d], zp[d - 1]))
    for cp in cps:
        cp.start()
    for cp in cps:
        cp.wait()
    acc = zat(zb, z)[...]
    for d in range(7):
        acc = acc + rx3[d]
    mine = zat(zo, z)
    mine[...] = acc
    cps = [rcopy(mine, mine, ss.at[19 + d], rs.at[19 + d], zp[d - 1]) for d in range(1, 8)]
    for cp in cps:
        cp.start()
    for cp in cps:
        cp.wait()
    h0 = m8(c * H)
    o_ref[pl.ds(h0 + a1, F), :] = zo[0:F, :]
    o_ref[pl.ds(h0 + b1, F), :] = zo[F : 2 * F, :]
    cps = []
    ra, rb = o_ref.at[pl.ds(h0 + a1, F)], o_ref.at[pl.ds(h0 + b1, F)]
    for d in range(1, 4):
        cps.append(rcopy(ra, ra, ss.at[26 + d], rs.at[26 + d], yp[d - 1]))
        cps.append(rcopy(rb, rb, ss.at[29 + d], rs.at[29 + d], xp[d - 1]))
    for cp in cps:
        cp.start()
    for cp in cps:
        cp.wait()
    cps = []
    ra, rb = o_ref.at[pl.ds(h0 + a0, E)], o_ref.at[pl.ds(h0 + b0, E)]
    for d in range(1, 4):
        cps.append(rcopy(ra, ra, ss.at[32 + d], rs.at[32 + d], xp[d - 1]))
        cps.append(rcopy(rb, rb, ss.at[35 + d], rs.at[35 + d], yp[d - 1]))
    for cp in cps:
        cp.start()
    for cp in cps:
        cp.wait()
    half = o_ref.at[pl.ds(h0, H)]
    cp = rcopy(half, half, ss.at[39], rs.at[39], core)
    cp.start()
    cp.wait()


def big_ar(v, cid):
    n = v.shape[0]
    H, E, F = n // 2, n // 16, n // 64
    return pl.pallas_call(
        functools.partial(big_kernel, n),
        out_shape=jax.ShapeDtypeStruct((n, 256), f32),
        in_specs=[pl.BlockSpec(memory_space=pltpu.VMEM)],
        out_specs=pl.BlockSpec(memory_space=pltpu.VMEM),
        scratch_shapes=[
            pltpu.VMEM((H, 256), f32),
            pltpu.VMEM((H, 256), f32),
            pltpu.VMEM((2, 3, E, 256), f32),
            pltpu.VMEM((2, 3, F, 256), f32),
            pltpu.VMEM((7, F // 2, 128), f32),
            pltpu.VMEM((2 * F, 256), f32),
            pltpu.VMEM((2 * F, 256), f32),
            pltpu.SemaphoreType.DMA((40,)),
            pltpu.SemaphoreType.DMA((40,)),
        ],
        compiler_params=pltpu.CompilerParams(
            collective_id=cid, has_side_effects=True, vmem_limit_bytes=40 * 2**20
        ),
    )(v)


D = 256
HEAD_COUNT = 8
SLICES = 64
HEAD_DIM = 32


def norm_rows(values, gain):
    centre = jnp.mean(values, axis=1, keepdims=True)
    centred = values - centre
    spread = jnp.mean(centred * centred, axis=1, keepdims=True)
    return (centred * lax.rsqrt(spread + 1e-05) * gain).astype(jnp.bfloat16)


def partition_share(
    incoming_entries,
    leading_scale_factor,
    intermediate_map_matrix,
    partitioned_map_matrix,
    partition_score_matrix,
    softening_factor,
):
    count = incoming_entries.shape[0]
    normed = norm_rows(incoming_entries, leading_scale_factor)
    middle = jnp.dot(normed, intermediate_map_matrix, preferred_element_type=jnp.float32).reshape(
        count, HEAD_COUNT, HEAD_DIM
    )
    feature = jnp.dot(normed, partitioned_map_matrix, preferred_element_type=jnp.float32).reshape(
        count, HEAD_COUNT, HEAD_DIM
    )
    partition_scores = jnp.einsum(
        "che,em->chm",
        middle,
        partition_score_matrix.astype(jnp.float32),
        precision=lax.Precision.HIGHEST,
    )
    exponentiated_scores = jnp.exp(partition_scores / softening_factor[None, :, None])
    partition_probabilities = exponentiated_scores / jnp.sum(
        exponentiated_scores, axis=2, keepdims=True
    )
    aggregated_states = jnp.einsum(
        "chm,che->hme", partition_probabilities, feature, precision=lax.Precision.HIGHEST
    )
    partition_mass = jnp.sum(partition_probabilities, axis=0)
    return (
        aggregated_states,
        partition_mass,
        partition_probabilities.reshape(count, HEAD_COUNT * SLICES),
    )


def token_mix(aggregated_states, partition_mass, asking_matrix, lookup_matrix, content_matrix):
    tokens = aggregated_states / partition_mass[:, :, None]
    queries = jnp.einsum(
        "hme,ef->hmf", tokens, asking_matrix.astype(jnp.float32), precision=lax.Precision.HIGHEST
    )
    key_rows = jnp.einsum(
        "hme,ef->hmf", tokens, lookup_matrix.astype(jnp.float32), precision=lax.Precision.HIGHEST
    )
    value_rows = jnp.einsum(
        "hme,ef->hmf", tokens, content_matrix.astype(jnp.float32), precision=lax.Precision.HIGHEST
    )
    scores = jnp.einsum(
        "hmf,hnf->hmn", queries, key_rows, precision=lax.Precision.HIGHEST
    ) * HEAD_DIM ** (-0.5)
    exponentiated_scores = jnp.exp(scores)
    probs = exponentiated_scores / jnp.sum(exponentiated_scores, axis=2, keepdims=True)
    return jnp.einsum("hmn,hnf->hmf", probs, value_rows, precision=lax.Precision.HIGHEST)


def mix_part(
    incoming_entries,
    partition_probabilities,
    mixed_tokens,
    result_matrix,
    trailing_scale_factor,
    expanding_matrix,
    contracting_matrix,
):
    count = incoming_entries.shape[0]
    spread = (
        jnp.einsum(
            "chm,hme->che",
            partition_probabilities.reshape(count, HEAD_COUNT, SLICES),
            mixed_tokens,
            precision=lax.Precision.HIGHEST,
        )
        .reshape(count, D)
        .astype(jnp.bfloat16)
    )
    state = incoming_entries + jnp.dot(spread, result_matrix, preferred_element_type=jnp.float32)
    normed = norm_rows(state, trailing_scale_factor)
    hidden = jax.nn.gelu(
        jnp.dot(normed, expanding_matrix, preferred_element_type=jnp.float32), approximate=True
    ).astype(jnp.bfloat16)
    return state + jnp.dot(hidden, contracting_matrix, preferred_element_type=jnp.float32)


def on_device(
    mesh_element_data,
    loss_sensitivity,
    leading_scale_factor,
    intermediate_map_matrix,
    partitioned_map_matrix,
    partition_score_matrix,
    softening_factor,
    asking_matrix,
    lookup_matrix,
    content_matrix,
    result_matrix,
    trailing_scale_factor,
    expanding_matrix,
    contracting_matrix,
):
    incoming_entries = mesh_element_data[0].astype(jnp.float32)
    dyrows = loss_sensitivity[0].astype(jnp.float32)
    firsts, reverse_opening_pass = jax.vjp(
        partition_share,
        incoming_entries,
        leading_scale_factor,
        intermediate_map_matrix,
        partitioned_map_matrix,
        partition_score_matrix,
        softening_factor,
    )
    aggregated_states, partition_mass, partition_probabilities = firsts
    rows = jnp.concatenate(
        [aggregated_states.reshape(8, 16, 128), jnp.pad(partition_mass.reshape(8, 1, 64), ((0, 0), (0, 7), (0, 64)))],
        axis=1,
    )
    rows = small_ar(rows, 0)
    aggregated_states = rows[:, :16].reshape(HEAD_COUNT, SLICES, HEAD_DIM)
    partition_mass = rows[:, 16, :64]
    mixed_tokens, back_mix = jax.vjp(
        token_mix, aggregated_states, partition_mass, asking_matrix, lookup_matrix, content_matrix
    )
    unused_y, back_two = jax.vjp(
        mix_part,
        incoming_entries,
        partition_probabilities,
        mixed_tokens,
        result_matrix,
        trailing_scale_factor,
        expanding_matrix,
        contracting_matrix,
    )
    dx_two, d_weights, d_tokens, g_out, g_gain_two, g_up, g_down = back_two(dyrows)
    d_tokens = small_ar(d_tokens.reshape(8, 16, 128), 1).reshape(HEAD_COUNT, SLICES, HEAD_DIM)
    d_weighted, d_totals, g_query, g_key, g_value = back_mix(d_tokens)
    dx_one, g_gain_one, g_mid, g_feat, g_slice, g_temp = reverse_opening_pass(
        (d_weighted, d_totals, d_weights)
    )
    grad_cells = (dx_one + dx_two).astype(jnp.bfloat16)[None]
    f32 = jnp.float32
    first = (lax.axis_index("point") == 0).astype(f32)
    smalls = (g_gain_one, g_slice.astype(f32), g_temp, g_gain_two) + tuple(
        t.astype(f32) * first for t in (g_query, g_key, g_value)
    )
    sizes = [t.size for t in smalls]
    flat = jnp.concatenate([t.reshape(-1) for t in smalls])
    flat = jnp.pad(flat, (0, 256 * 256 - flat.size)).reshape(256, 256)
    up = g_up.astype(f32)
    stack = jnp.concatenate(
        [g_down.astype(f32)]
        + [up[:, k * 256 : (k + 1) * 256] for k in range(4)]
        + [g_out.astype(f32), g_mid.astype(f32), g_feat.astype(f32), flat]
    )
    stack = big_ar(stack, 2)
    flat = stack[2816:].reshape(-1)
    parts, at = [], 0
    for t, size in zip(smalls, sizes):
        parts.append(flat[at : at + size].reshape(t.shape))
        at += size
    up = jnp.concatenate([stack[1024 + k * 256 : 1280 + k * 256] for k in range(4)], axis=1)
    summed = (
        parts[0], stack[2304:2560], stack[2560:2816], parts[1], parts[2],
        stack[2048:2304], parts[3], up, stack[:1024],
    )
    mixed = parts[4:]
    derivative_collection = (
        summed[0],
        summed[1],
        summed[2],
        summed[3],
        summed[4],
        mixed[0],
        mixed[1],
        mixed[2],
        summed[5],
        summed[6],
        summed[7],
        summed[8],
    )
    return (
        grad_cells,
        derivative_collection[0],
        derivative_collection[1],
        derivative_collection[2],
        derivative_collection[3],
        derivative_collection[4],
        derivative_collection[5],
        derivative_collection[6],
        derivative_collection[7],
        derivative_collection[8],
        derivative_collection[9],
        derivative_collection[10],
        derivative_collection[11],
    )


def solution(mesh):
    return jax.shard_map(
        on_device,
        mesh=mesh,
        in_specs=(
            P("dp", "point", None),
            P("dp", "point", None),
            P(),
            P(),
            P(),
            P(),
            P(),
            P(),
            P(),
            P(),
            P(),
            P(),
            P(),
            P(),
        ),
        out_specs=(
            P("dp", "point", None),
            P(),
            P(),
            P(),
            P(),
            P(),
            P(),
            P(),
            P(),
            P(),
            P(),
            P(),
            P(),
        ),
        check_vma=False,
    )
```

```python
import functools
import jax
import jax.numpy as jnp
from jax import lax
from jax.experimental import pallas as pl
from jax.experimental.pallas import tpu as pltpu
from jax.sharding import PartitionSpec as P

MESH = pl.DeviceIdType.MESH
HIGHEST = lax.Precision.HIGHEST
f32 = jnp.float32
bf16 = jnp.bfloat16

CELLS = 768
D = 256
FF = 1024
HEADS = 8
SLICES = 64
HEAD_DIM = 32
HM = HEADS * SLICES
TILE = 256
EPS = 1e-05
N1 = 2048
N2 = 1024
SMALL = 768
GELU_C = 0.7978845608028654
GELU_A = 0.044715


def rcopy(src, dst, ss, rs, dev):
    return pltpu.make_async_remote_copy(
        src_ref=src, dst_ref=dst, send_sem=ss, recv_sem=rs, device_id=dev, device_id_type=MESH
    )


def m8(v):
    return pl.multiple_of(v, 8)


class Place:
    def __init__(self):
        self.y = lax.axis_index("dp")
        p = lax.axis_index("point")
        self.z = p // 8
        self.g = lax.rem(p, 8)
        self.x = self.g // 2
        self.c = lax.rem(self.g, 2)
        z, x, c, g, y = self.z, self.x, self.c, self.g, self.y
        self.core = {"point": z * 8 + x * 2 + (1 - c)}
        self.gp = [{"point": z * 8 + lax.rem(g + d, 8)} for d in range(1, 8)]
        self.zp = [{"point": lax.rem(z + d, 8) * 8 + g} for d in range(1, 8)]
        self.xp = [{"point": z * 8 + lax.rem(x + d, 4) * 2 + c} for d in range(1, 4)]
        self.yp = [{"dp": lax.rem(y + d, 4)} for d in range(1, 4)]


class SmallSum:
    def __init__(self, at, s, o, rx1, rx2, ss, rs):
        self.at, self.s, self.o, self.rx1, self.rx2, self.ss, self.rs = at, s, o, rx1, rx2, ss, rs
        self.stage = 0
        self.copies = []

    def wait(self):
        for cp in self.copies:
            cp.wait()
        self.copies = []

    def step(self):
        at, s, o, rx1, rx2, ss, rs = self.at, self.s, self.o, self.rx1, self.rx2, self.ss, self.rs
        self.wait()
        k = self.stage
        self.stage += 1
        if k == 0:
            for d in range(1, 8):
                src = s.at[lax.rem(at.g + d, 8)]
                self.copies.append(rcopy(src, rx1.at[d - 1], ss.at[0, d - 1], rs.at[0, d - 1], at.gp[d - 1]))
        elif k == 1:
            acc = s[at.g]
            for d in range(7):
                acc = acc + rx1[d]
            rx2[at.z] = acc
            mine = rx2.at[at.z]
            for d in range(1, 8):
                self.copies.append(rcopy(mine, mine, ss.at[1, d - 1], rs.at[1, d - 1], at.zp[d - 1]))
        elif k == 2:
            acc = rx2[0]
            for d in range(1, 8):
                acc = acc + rx2[d]
            o[at.g] = acc
            mine = o.at[at.g]
            for d in range(1, 8):
                self.copies.append(rcopy(mine, mine, ss.at[2, d - 1], rs.at[2, d - 1], at.gp[d - 1]))
        for cp in self.copies:
            cp.start()


def add_rows(dst, d0, base, b0, srcs, rows):
    t = min(rows, 64)

    def body(i, _):
        o = pl.multiple_of(i * t, t)
        acc = base[pl.ds(m8(b0 + o), t), :]
        for s in srcs:
            acc = acc + s[pl.ds(o, t), :]
        dst[pl.ds(m8(d0 + o), t), :] = acc
        return 0

    lax.fori_loop(0, rows // t, body, 0)


class BigSum:
    def __init__(self, n, at, src, o, bufs, ss, rs):
        self.n, self.at, self.src, self.o, self.ss, self.rs = n, at, src, o, ss, rs
        self.gref, self.rx0, self.rx1, self.rx2, self.rx3, self.zb, self.zo = bufs
        self.H, self.Q, self.E, self.F = n // 2, n // 4, n // 16, n // 64
        self.K = self.F // 2
        E, F, Q, H = self.E, self.F, self.Q, self.H
        self.h0 = m8(at.c * H)
        self.a0, self.b0 = m8(at.x * E), m8(Q + at.y * E)
        self.a1, self.b1 = m8(self.a0 + at.y * F), m8(self.b0 + at.x * F)
        self.stage = 0
        self.copies = []
        self.sem = 0

    def add(self, src, dst, dev):
        self.copies.append(rcopy(src, dst, self.ss.at[self.sem], self.rs.at[self.sem], dev))
        self.sem += 1

    def zat(self, ref, k):
        K = self.K
        return ref.at[pl.ds(m8((k // 2) * K), K), pl.ds(pl.multiple_of(lax.rem(k, 2) * 128, 128), 128)]

    def step(self):
        at, H, Q, E, F = self.at, self.H, self.Q, self.E, self.F
        gref, rx0, rx1, rx2, rx3, zb, zo, o = (
            self.gref, self.rx0, self.rx1, self.rx2, self.rx3, self.zb, self.zo, self.o,
        )
        h0, a0, b0, a1, b1 = self.h0, self.a0, self.b0, self.a1, self.b1
        for cp in self.copies:
            cp.wait()
        self.copies = []
        k = self.stage
        self.stage += 1
        if k == 0:
            self.add(self.src.at[pl.ds(m8((1 - at.c) * H), H)], rx0, at.core)
        elif k == 1:
            add_rows(gref, 0, self.src, h0, [rx0], H)
            for d in range(1, 4):
                xi, yi = lax.rem(at.x + d, 4), lax.rem(at.y + d, 4)
                self.add(gref.at[pl.ds(m8(xi * E), E)], rx1.at[0, d - 1], at.xp[d - 1])
                self.add(gref.at[pl.ds(m8(Q + yi * E), E)], rx1.at[1, d - 1], at.yp[d - 1])
        elif k == 2:
            add_rows(gref, a0, gref, a0, [rx1.at[0, d] for d in range(3)], E)
            add_rows(gref, b0, gref, b0, [rx1.at[1, d] for d in range(3)], E)
            for d in range(1, 4):
                xi, yi = lax.rem(at.x + d, 4), lax.rem(at.y + d, 4)
                self.add(gref.at[pl.ds(m8(a0 + yi * F), F)], rx2.at[0, d - 1], at.yp[d - 1])
                self.add(gref.at[pl.ds(m8(b0 + xi * F), F)], rx2.at[1, d - 1], at.xp[d - 1])
        elif k == 3:
            add_rows(zb, 0, gref, a1, [rx2.at[0, d] for d in range(3)], F)
            add_rows(zb, F, gref, b1, [rx2.at[1, d] for d in range(3)], F)
            for d in range(1, 8):
                self.add(self.zat(zb, lax.rem(at.z + d, 8)), rx3.at[d - 1], at.zp[d - 1])
        elif k == 4:
            acc = self.zat(zb, at.z)[...]
            for d in range(7):
                acc = acc + rx3[d]
            mine = self.zat(zo, at.z)
            mine[...] = acc
            for d in range(1, 8):
                self.add(mine, mine, at.zp[d - 1])
        elif k == 5:
            o[pl.ds(m8(h0 + a1), F), :] = zo[0:F, :]
            o[pl.ds(m8(h0 + b1), F), :] = zo[F : 2 * F, :]
            ra, rb = o.at[pl.ds(m8(h0 + a1), F)], o.at[pl.ds(m8(h0 + b1), F)]
            for d in range(1, 4):
                self.add(ra, ra, at.yp[d - 1])
                self.add(rb, rb, at.xp[d - 1])
        elif k == 6:
            ra, rb = o.at[pl.ds(m8(h0 + a0), E)], o.at[pl.ds(m8(h0 + b0), E)]
            for d in range(1, 4):
                self.add(ra, ra, at.xp[d - 1])
                self.add(rb, rb, at.yp[d - 1])
        elif k == 7:
            half = o.at[pl.ds(h0, H)]
            self.add(half, half, at.core)
        for cp in self.copies:
            cp.start()


def small_scratch(r):
    return [
        pltpu.VMEM((8, r, 128), f32),
        pltpu.VMEM((8, r, 128), f32),
        pltpu.VMEM((7, r, 128), f32),
        pltpu.VMEM((8, r, 128), f32),
        pltpu.SemaphoreType.DMA((3, 7)),
        pltpu.SemaphoreType.DMA((3, 7)),
    ]


def big_scratch(n):
    H, E, F = n // 2, n // 16, n // 64
    return [
        pltpu.VMEM((n, 256), f32),
        pltpu.VMEM((H, 256), f32),
        pltpu.VMEM((H, 256), f32),
        pltpu.VMEM((2, 3, E, 256), f32),
        pltpu.VMEM((2, 3, F, 256), f32),
        pltpu.VMEM((7, F // 2, 128), f32),
        pltpu.VMEM((2 * F, 256), f32),
        pltpu.VMEM((2 * F, 256), f32),
        pltpu.SemaphoreType.DMA((40,)),
        pltpu.SemaphoreType.DMA((40,)),
    ]


def dg(a, b, ca, cb, precision=None):
    return lax.dot_general(a, b, (((ca,), (cb,)), ((), ())), preferred_element_type=f32, precision=precision)


def exact(a, b, ca, cb):
    return dg(a, b, ca, cb, HIGHEST)


def split(v):
    hi = v.astype(bf16)
    return hi, (v - hi.astype(f32)).astype(bf16)


def iota(shape, dim):
    return lax.broadcasted_iota(jnp.int32, shape, dim)


def block_sum(v, ones):
    out = []
    for half in range(2):
        hi, lo = split(v[:, half * 256 : (half + 1) * 256])
        out.append(dg(hi, ones, 1, 0) + dg(lo, ones, 1, 0))
    return jnp.concatenate(out, axis=1)


def spread_heads(t):
    lanes = iota((HEAD_DIM, HM), 1) // SLICES
    return jnp.concatenate([jnp.where(lanes == h, t, 0.0) for h in range(HEADS)], axis=0)


def gather_heads(ref):
    lanes = iota((HEAD_DIM, HM), 1) // SLICES
    acc = jnp.zeros((HEAD_DIM, HM), f32)
    for h in range(HEADS):
        acc = jnp.where(lanes == h, ref[h * HEAD_DIM : (h + 1) * HEAD_DIM, :], acc)
    return acc


def mean_rows(v):
    return jnp.sum(v, axis=1, keepdims=True) * (1.0 / D)


def norm_parts(v):
    centred = v - mean_rows(v)
    rstd = lax.rsqrt(mean_rows(centred * centred) + EPS)
    return centred * rstd, rstd


def norm_back(dn, xhat, rstd, gain):
    dxh = dn * gain
    return rstd * (dxh - mean_rows(dxh) - xhat * mean_rows(dxh * xhat))


def fold8(v):
    return jnp.sum(v.reshape(v.shape[0] // 8, 8, v.shape[1]), axis=0)


def tiles(body):
    def step(i, _):
        body(pl.ds(pl.multiple_of(i * TILE, TILE), TILE))
        return 0

    lax.fori_loop(0, CELLS // TILE, step, 0)


def main_kernel(
    temp_ref, x_ref, dy_ref, gain1_ref, wmid_ref, wfeat_ref, ws_ref, wq_ref, wk_ref, wv_ref, wout_ref, gain2_ref,
    wup_ref, wdown_ref,
    cells_ref, o1_ref, o2_ref,
    normed_ref, mid_ref, feat_ref, l_ref, w_ref, wb_ref, spread_ref, normed2_ref, hidden_ref, du_ref, dstate_ref,
    dsb_ref, dsp_ref, dw2_ref, bds_ref, bdm_ref, bdw_ref, big_acc, mid_acc, row_acc, p_ref,
    s1, so1, s1a, s1b, ss1, rs1, s2, so2, s2a, s2b, ss2, rs2,
    g1, g1a, g1b, g1c, g1d, g1e, g1f, g1g, ss3, rs3, g2, g2a, g2b, g2c, g2d, g2e, g2f, g2g, ss4, rs4,
):
    at = Place()
    everyone = at.gp + at.zp + at.yp
    sem = pltpu.get_barrier_semaphore()
    for dev in everyone:
        pl.semaphore_signal(sem, inc=1, device_id=dev, device_id_type=MESH)
    sum1 = SmallSum(at, s1, so1, s1a, s1b, ss1, rs1)
    sum2 = SmallSum(at, s2, so2, s2a, s2b, ss2, rs2)
    big1 = BigSum(N1, at, g1, o1_ref, (g1a, g1b, g1c, g1d, g1e, g1f, g1g), ss3, rs3)
    big2 = BigSum(N2, at, g2, o2_ref, (g2a, g2b, g2c, g2d, g2e, g2f, g2g), ss4, rs4)

    head_of_lane = iota((1, HM), 1) // SLICES
    temp = jnp.zeros((1, HM), f32)
    for h in range(HEADS):
        temp = jnp.where(head_of_lane == h, temp_ref[h], temp)
    inv_temp = 1.0 / temp
    ones = (iota((256, 256), 0) // SLICES == iota((256, 256), 1) // SLICES).astype(f32).astype(bf16)
    place = (iota((SLICES, HM), 0) == lax.rem(iota((SLICES, HM), 1), SLICES)).astype(f32)
    wide = dg(ws_ref[...], place.astype(bf16), 1, 0)
    bds_ref[...] = spread_heads(wide).astype(bf16)
    gain1 = gain1_ref[...]
    gain2 = gain2_ref[...]

    big_acc[...] = jnp.zeros_like(big_acc)
    row_acc[...] = jnp.zeros_like(row_acc)

    def part_a(r):
        xhat, _ = norm_parts(x_ref[r, :].astype(f32))
        normed = (xhat * gain1).astype(bf16)
        normed_ref[r, :] = normed
        mid = dg(normed, wmid_ref[...], 1, 0)
        feat = dg(normed, wfeat_ref[...], 1, 0).astype(bf16)
        hi, lo = split(mid)
        mid_ref[r, :] = hi
        feat_ref[r, :] = feat
        logits = (dg(hi, bds_ref[...], 1, 0) + dg(lo, bds_ref[...], 1, 0)) * inv_temp
        l_ref[r, :] = logits
        e = jnp.exp(logits)
        w = e / block_sum(e, ones)
        w_ref[r, :] = w
        wb = w.astype(bf16)
        wb_ref[r, :] = wb
        big_acc[...] += dg(feat, wb, 0, 0)
        row_acc[...] += fold8(w)

    tiles(part_a)
    tt = gather_heads(big_acc)
    tot = row_acc[...]
    for j in range(8):
        lanes = slice((j // 2) * 128, (j // 2 + 1) * 128)
        s1[j, 0:16, :] = tt[(j % 2) * 16 : (j % 2 + 1) * 16, lanes]
        s1[j, 16:24, :] = tot[:, lanes]

    pl.semaphore_wait(sem, len(everyone))
    sum1.step()
    sum1.step()
    sum1.step()
    sum1.wait()

    wq, wk, wv = (r[...].astype(f32) for r in (wq_ref, wk_ref, wv_ref))
    scale = HEAD_DIM**-0.5
    same = iota((128, 128), 0) // SLICES == iota((128, 128), 1) // SLICES
    mix = []
    kept = []
    for b in range(4):
        total = jnp.sum(so1[2 * b, 16:24, :], axis=0, keepdims=True)
        tok = jnp.concatenate([so1[2 * b, 0:16, :], so1[2 * b + 1, 0:16, :]], axis=0) / total
        q = exact(wq, tok, 0, 0)
        k = exact(wk, tok, 0, 0)
        v = exact(wv, tok, 0, 0)
        sc = exact(q, k, 0, 0) * scale
        e = jnp.where(same, jnp.exp(jnp.where(same, sc, 0.0)), 0.0)
        prob = e / jnp.sum(e, axis=1, keepdims=True)
        p_ref[b] = prob
        mix.append(exact(v, prob, 1, 1))
        kept.append((total, tok, q, k, v))
    hi, lo = split(spread_heads(jnp.concatenate(mix, axis=1)))
    bdm_ref[0] = hi
    bdm_ref[1] = lo

    big_acc[...] = jnp.zeros_like(big_acc)
    row_acc[...] = jnp.zeros_like(row_acc)

    def part_b(r):
        wb = wb_ref[r, :]
        sp = (dg(wb, bdm_ref[0], 1, 1) + dg(wb, bdm_ref[1], 1, 1)).astype(bf16)
        spread_ref[r, :] = sp
        state = x_ref[r, :].astype(f32) + dg(sp, wout_ref[...], 1, 0)
        xhat, rstd = norm_parts(state)
        normed = (xhat * gain2).astype(bf16)
        normed2_ref[r, :] = normed
        dy = dy_ref[r, :]
        dn = jnp.zeros((TILE, D), f32)
        for j in range(4):
            cols = slice(j * 256, (j + 1) * 256)
            u = dg(normed, wup_ref[:, cols], 1, 0)
            u2 = u * u
            t = jnp.tanh(u * (GELU_C + (GELU_C * GELU_A) * u2))
            half = 0.5 + 0.5 * t
            hidden_ref[r, cols] = (u * half).astype(bf16)
            slope = half + u * half * (1.0 - t) * (GELU_C + (3.0 * GELU_C * GELU_A) * u2)
            dh = dg(dy, wdown_ref[cols, :], 1, 1).astype(bf16).astype(f32)
            du = (dh * slope).astype(bf16)
            du_ref[r, cols] = du
            dn = dn + dg(du, wup_ref[:, cols], 1, 1)
        dn = dn.astype(bf16).astype(f32)
        row_acc[:, 0:256] += fold8(dn * xhat)
        ds = dy.astype(f32) + norm_back(dn, xhat, rstd, gain2)
        dstate_ref[r, :] = ds
        dsb = ds.astype(bf16)
        dsb_ref[r, :] = dsb
        dsp = dg(dsb, wout_ref[...], 1, 1).astype(bf16)
        dsp_ref[r, :] = dsp
        big_acc[...] += dg(dsp, wb, 0, 0)

    tiles(part_b)
    dmt = gather_heads(big_acc)
    for j in range(8):
        s2[j] = dmt[(j % 2) * 16 : (j % 2 + 1) * 16, (j // 2) * 128 : (j // 2 + 1) * 128]
    g_gain2 = jnp.sum(row_acc[:, 0:256], axis=0, keepdims=True)
    sum2.step()

    for j in range(4):
        cols = slice(j * 256, (j + 1) * 256)
        g1[j * 256 : (j + 1) * 256, :] = dg(hidden_ref[:, cols], dy_ref[...], 0, 0)
    sum2.step()
    for j in range(4):
        cols = slice(j * 256, (j + 1) * 256)
        g1[1024 + j * 256 : 1280 + j * 256, :] = dg(normed2_ref[...], du_ref[:, cols], 0, 0)
    big1.step()

    def part_dw(r):
        dsp = dsp_ref[r, :]
        dw2_ref[r, :] = dg(dsp, bdm_ref[0], 1, 0) + dg(dsp, bdm_ref[1], 1, 0)

    tiles(part_dw)
    g2[512:768, :] = dg(spread_ref[...], dsb_ref[...], 0, 0)
    sum2.step()
    big1.step()
    sum2.wait()

    gq = jnp.zeros((HEAD_DIM, HEAD_DIM), f32)
    gk, gv = gq, gq
    dwt, dtot = [], []
    for b in range(4):
        total, tok, q, k, v = kept[b]
        prob = p_ref[b]
        dm = jnp.concatenate([so2[2 * b], so2[2 * b + 1]], axis=0)
        dp = exact(dm, v, 0, 0)
        dsc = prob * (dp - jnp.sum(prob * dp, axis=1, keepdims=True)) * scale
        dq = exact(k, dsc, 1, 1)
        dk = exact(q, dsc, 1, 0)
        dv = exact(dm, prob, 1, 0)
        gq = gq + exact(tok, dq, 1, 1)
        gk = gk + exact(tok, dk, 1, 1)
        gv = gv + exact(tok, dv, 1, 1)
        dtok = exact(wq, dq, 1, 0) + exact(wk, dk, 1, 0) + exact(wv, dv, 1, 0)
        dtok = dtok / total
        dwt.append(dtok)
        dtot.append(-jnp.sum(dtok * tok, axis=0, keepdims=True))
    hi, lo = split(spread_heads(jnp.concatenate(dwt, axis=1)))
    bdw_ref[0] = hi
    bdw_ref[1] = lo
    d_totals = jnp.concatenate(dtot, axis=1)

    big_acc[...] = jnp.zeros_like(big_acc)
    mid_acc[...] = jnp.zeros_like(mid_acc)
    row_acc[...] = jnp.zeros_like(row_acc)
    g2[0:512, :] = jnp.zeros((512, 256), f32)

    def part_c(r):
        w = w_ref[r, :]
        wb = wb_ref[r, :]
        feat = feat_ref[r, :]
        normed = normed_ref[r, :]
        dfeat = (dg(wb, bdw_ref[0], 1, 1) + dg(wb, bdw_ref[1], 1, 1)).astype(bf16)
        dw = dw2_ref[r, :] + dg(feat, bdw_ref[0], 1, 0) + dg(feat, bdw_ref[1], 1, 0) + d_totals
        dl = w * (dw - block_sum(w * dw, ones))
        row_acc[...] += fold8(dl * l_ref[r, :])
        dlt = (dl * inv_temp).astype(bf16)
        dmid = dg(dlt, bds_ref[...], 1, 1).astype(bf16)
        big_acc[...] += dg(mid_ref[r, :], dlt, 0, 0)
        g2[0:256, :] += dg(normed, dfeat, 0, 0)
        g2[256:512, :] += dg(normed, dmid, 0, 0)
        dn = dg(dmid, wmid_ref[...], 1, 1).astype(bf16).astype(f32) + dg(dfeat, wfeat_ref[...], 1, 1).astype(
            bf16
        ).astype(f32)
        dn = dn.astype(bf16).astype(f32)
        xhat, rstd = norm_parts(x_ref[r, :].astype(f32))
        mid_acc[...] += fold8(dn * xhat)
        cells_ref[r, :] = (norm_back(dn, xhat, rstd, gain1) + dstate_ref[r, :]).astype(bf16)

    tiles(part_c)
    big1.step()

    first = (lax.axis_index("point") == 0).astype(f32)
    g2[SMALL:N2, :] = jnp.zeros((N2 - SMALL, 256), f32)
    pick = (iota((HM, 256), 0) // SLICES == iota((HM, 256), 1)).astype(f32)
    inv8 = jnp.zeros((1, 256), f32)
    for h in range(HEADS):
        inv8 = jnp.where(iota((1, 256), 1) == h, 1.0 / temp_ref[h], inv8)
    g_temp = jnp.sum(exact(row_acc[...], pick, 1, 0), axis=0, keepdims=True) * (-inv8)
    g2[SMALL : SMALL + 1, :] = jnp.sum(mid_acc[...], axis=0, keepdims=True)
    g2[SMALL + 1 : SMALL + 2, :] = g_gain2
    g2[SMALL + 2 : SMALL + 3, :] = g_temp
    g2[SMALL + 8 : SMALL + 40, 0:64] = exact(gather_heads(big_acc), place, 1, 1)
    g2[SMALL + 8 : SMALL + 40, 128:160] = gq * first
    g2[SMALL + 40 : SMALL + 72, 0:32] = gk * first
    g2[SMALL + 40 : SMALL + 72, 128:160] = gv * first
    big2.step()
    for _ in range(4):
        big1.step()
        big2.step()
    big1.step()
    big2.step()
    big1.step()
    big2.step()
    big2.step()
    big2.step()
    big2.step()


def out_kernel(
    cells_ref, o1, o2, cells_out, gain1, mid, feat, slc, temp, wq, wk, wv, wout, gain2, up, down,
):
    cells_out[...] = cells_ref[...]
    down[...] = o1[0:1024, :]
    for j in range(4):
        up[:, j * 256 : (j + 1) * 256] = o1[1024 + j * 256 : 1280 + j * 256, :]
    feat[...] = o2[0:256, :]
    mid[...] = o2[256:512, :]
    wout[...] = o2[512:768, :]
    gain1[...] = o2[SMALL : SMALL + 1, :]
    gain2[...] = o2[SMALL + 1 : SMALL + 2, :]
    temp[...] = o2[SMALL + 2 : SMALL + 3, 0:8]
    slc[...] = o2[SMALL + 8 : SMALL + 40, 0:64]
    wq[...] = o2[SMALL + 8 : SMALL + 40, 128:160]
    wk[...] = o2[SMALL + 40 : SMALL + 72, 0:32]
    wv[...] = o2[SMALL + 40 : SMALL + 72, 128:160]


def vmem(count):
    return [pl.BlockSpec(memory_space=pltpu.VMEM)] * count


def on_device(x, dy, gain1, wmid, wfeat, ws, temp, wq, wk, wv, wout, gain2, wup, wdown):
    sds = jax.ShapeDtypeStruct
    cells, o1, o2 = pl.pallas_call(
        main_kernel,
        out_shape=(sds((CELLS, D), bf16), sds((N1, 256), f32), sds((N2, 256), f32)),
        in_specs=[pl.BlockSpec(memory_space=pltpu.SMEM)] + vmem(13),
        out_specs=vmem(3),
        scratch_shapes=[
            pltpu.VMEM((CELLS, D), bf16),
            pltpu.VMEM((CELLS, D), bf16),
            pltpu.VMEM((CELLS, D), bf16),
            pltpu.VMEM((CELLS, HM), f32),
            pltpu.VMEM((CELLS, HM), f32),
            pltpu.VMEM((CELLS, HM), bf16),
            pltpu.VMEM((CELLS, D), bf16),
            pltpu.VMEM((CELLS, D), bf16),
            pltpu.VMEM((CELLS, FF), bf16),
            pltpu.VMEM((CELLS, FF), bf16),
            pltpu.VMEM((CELLS, D), f32),
            pltpu.VMEM((CELLS, D), bf16),
            pltpu.VMEM((CELLS, D), bf16),
            pltpu.VMEM((CELLS, HM), f32),
            pltpu.VMEM((D, HM), bf16),
            pltpu.VMEM((2, D, HM), bf16),
            pltpu.VMEM((2, D, HM), bf16),
            pltpu.VMEM((D, HM), f32),
            pltpu.VMEM((8, D), f32),
            pltpu.VMEM((8, HM), f32),
            pltpu.VMEM((4, 128, 128), f32),
        ]
        + small_scratch(24)
        + small_scratch(16)
        + big_scratch(N1)
        + big_scratch(N2),
        compiler_params=pltpu.CompilerParams(
            collective_id=0, has_side_effects=True, vmem_limit_bytes=56 * 2**20
        ),
    )(
        temp, x[0], dy[0], gain1.reshape(1, D), wmid, wfeat, ws, wq, wk, wv, wout, gain2.reshape(1, D), wup, wdown,
    )
    outs = pl.pallas_call(
        out_kernel,
        out_shape=(
            sds((CELLS, D), bf16), sds((1, D), f32), sds((D, D), f32), sds((D, D), f32),
            sds((HEAD_DIM, SLICES), f32), sds((1, HEADS), f32), sds((HEAD_DIM, HEAD_DIM), f32),
            sds((HEAD_DIM, HEAD_DIM), f32), sds((HEAD_DIM, HEAD_DIM), f32), sds((D, D), f32), sds((1, D), f32),
            sds((D, FF), f32), sds((FF, D), f32),
        ),
        in_specs=vmem(3),
        out_specs=vmem(13),
        compiler_params=pltpu.CompilerParams(vmem_limit_bytes=24 * 2**20),
    )(cells, o1, o2)
    outs = list(outs)
    outs[0] = outs[0][None]
    outs[1] = outs[1].reshape(D)
    outs[5] = outs[5].reshape(HEADS)
    outs[10] = outs[10].reshape(D)
    return tuple(outs)


def solution(mesh):
    return jax.shard_map(
        on_device,
        mesh=mesh,
        in_specs=(P("dp", "point", None), P("dp", "point", None)) + (P(),) * 12,
        out_specs=(P("dp", "point", None),) + (P(),) * 12,
        check_vma=False,
    )
```

```python
import functools
import jax
import jax.numpy as jnp
from jax import lax
from jax.experimental import pallas as pl
from jax.experimental.pallas import tpu as pltpu
from jax.sharding import PartitionSpec as P

MESH = pl.DeviceIdType.MESH
HIGHEST = lax.Precision.HIGHEST
f32 = jnp.float32
bf16 = jnp.bfloat16

CELLS = 768
D = 256
FF = 1024
HEADS = 8
SLICES = 64
HEAD_DIM = 32
HM = HEADS * SLICES
EPS = 1e-05
N1 = 2048
N2 = 512
N3 = 384
SMALL = 256
GELU_C = 0.7978845608028654
GELU_A = 0.044715


def rcopy(src, dst, ss, rs, dev):
    return pltpu.make_async_remote_copy(
        src_ref=src, dst_ref=dst, send_sem=ss, recv_sem=rs, device_id=dev, device_id_type=MESH
    )


def m8(v):
    return pl.multiple_of(v, 8)


class Place:
    def __init__(self):
        self.y = lax.axis_index("dp")
        p = lax.axis_index("point")
        self.z = p // 8
        self.g = lax.rem(p, 8)
        self.x = self.g // 2
        self.c = lax.rem(self.g, 2)
        z, x, c, g, y = self.z, self.x, self.c, self.g, self.y
        self.core = {"point": z * 8 + x * 2 + (1 - c)}
        self.gp = [{"point": z * 8 + lax.rem(g + d, 8)} for d in range(1, 8)]
        self.zp = [{"point": lax.rem(z + d, 8) * 8 + g} for d in range(1, 8)]
        self.xp = [{"point": z * 8 + lax.rem(x + d, 4) * 2 + c} for d in range(1, 4)]
        self.yp = [{"dp": lax.rem(y + d, 4)} for d in range(1, 4)]
        self.xyp = [
            {"dp": lax.rem(y + d % 4, 4), "point": z * 8 + lax.rem(x + d // 4, 4) * 2 + c} for d in range(1, 16)
        ]
        far = [self.xyp[d - 1] for d in range(1, 16) if d % 4]
        self.everyone = self.gp + self.zp + far


class Stage:
    def __init__(self, ss, rs):
        self.ss, self.rs, self.k, self.pending = ss, rs, -1, None
        self.copies = []

    def wait(self):
        if self.pending is not None:
            self.pending.wait_send()
            self.pending.wait_recv()
        self.pending = None
        self.copies = []

    def begin(self):
        self.wait()
        self.k += 1
        return self.k

    def add(self, src, dst, dev):
        rcopy(src, dst, self.ss.at[self.k], self.rs.at[self.k], dev).start()

    def total(self, ref, dev):
        self.pending = rcopy(ref, ref, self.ss.at[self.k], self.rs.at[self.k], dev)


class SmallSum(Stage):
    def __init__(self, at, s, o, rx1, rx2, ss, rs):
        super().__init__(ss, rs)
        self.at, self.s, self.o, self.rx1, self.rx2 = at, s, o, rx1, rx2

    def step(self):
        at, s, o, rx1, rx2 = self.at, self.s, self.o, self.rx1, self.rx2
        k = self.begin()
        if k == 0:
            for d in range(1, 8):
                self.add(s.at[lax.rem(at.g + d, 8)], rx1.at[d - 1], at.gp[d - 1])
            self.total(rx1, at.gp[0])
        elif k == 1:
            acc = s[at.g]
            for d in range(7):
                acc = acc + rx1[d]
            rx2[at.z] = acc
            mine = rx2.at[at.z]
            for d in range(7):
                self.add(mine, mine, at.zp[d])
            self.total(rx1, at.zp[0])
        elif k == 2:
            acc = rx2[0]
            for d in range(1, 8):
                acc = acc + rx2[d]
            o[at.g] = acc
            mine = o.at[at.g]
            for d in range(7):
                self.add(mine, mine, at.gp[d])
            self.total(rx1, at.gp[0])


def add_rows(dst, d0, base, b0, srcs, rows):
    t = min(rows, 64)

    def body(i, _):
        o = pl.multiple_of(i * t, t)
        acc = base[pl.ds(m8(b0 + o), t), :]
        for s in srcs:
            acc = acc + s[pl.ds(o, t), :]
        dst[pl.ds(m8(d0 + o), t), :] = acc
        return 0

    lax.fori_loop(0, rows // t, body, 0)


class BigSum(Stage):
    def __init__(self, n, at, src, o, bufs, ss, rs):
        super().__init__(ss, rs)
        self.n, self.at, self.src, self.o = n, at, src, o
        self.gref, self.rx0, self.rx1, self.rx2, self.rx3, self.zb, self.zo = bufs
        self.H, self.Q, self.E, self.F = n // 2, n // 4, n // 16, n // 64
        self.K = self.F // 2
        E, F, Q, H = self.E, self.F, self.Q, self.H
        self.h0 = m8(at.c * H)
        self.a0, self.b0 = m8(at.x * E), m8(Q + at.y * E)
        self.a1, self.b1 = m8(self.a0 + at.y * F), m8(self.b0 + at.x * F)

    def zat(self, ref, k):
        K = self.K
        return ref.at[pl.ds(m8((k // 2) * K), K), pl.ds(pl.multiple_of(lax.rem(k, 2) * 128, 128), 128)]

    def step(self):
        at, H, Q, E, F = self.at, self.H, self.Q, self.E, self.F
        gref, rx0, rx1, rx2, rx3, zb, zo, o = (
            self.gref, self.rx0, self.rx1, self.rx2, self.rx3, self.zb, self.zo, self.o,
        )
        h0, a0, b0, a1, b1 = self.h0, self.a0, self.b0, self.a1, self.b1
        k = self.begin()
        if k == 0:
            self.add(self.src.at[pl.ds(m8((1 - at.c) * H), H)], rx0, at.core)
            self.total(rx0, at.core)
        elif k == 1:
            add_rows(gref, 0, self.src, h0, [rx0], H)
            for d in range(1, 4):
                xi, yi = lax.rem(at.x + d, 4), lax.rem(at.y + d, 4)
                self.add(gref.at[pl.ds(m8(xi * E), E)], rx1.at[0, d - 1], at.xp[d - 1])
                self.add(gref.at[pl.ds(m8(Q + yi * E), E)], rx1.at[1, d - 1], at.yp[d - 1])
            self.total(rx1, at.xp[0])
        elif k == 2:
            add_rows(gref, a0, gref, a0, [rx1.at[0, d] for d in range(3)], E)
            add_rows(gref, b0, gref, b0, [rx1.at[1, d] for d in range(3)], E)
            for d in range(1, 4):
                xi, yi = lax.rem(at.x + d, 4), lax.rem(at.y + d, 4)
                self.add(gref.at[pl.ds(m8(a0 + yi * F), F)], rx2.at[0, d - 1], at.yp[d - 1])
                self.add(gref.at[pl.ds(m8(b0 + xi * F), F)], rx2.at[1, d - 1], at.xp[d - 1])
            self.total(rx2, at.xp[0])
        elif k == 3:
            add_rows(zb, 0, gref, a1, [rx2.at[0, d] for d in range(3)], F)
            add_rows(zb, F, gref, b1, [rx2.at[1, d] for d in range(3)], F)
            for d in range(1, 8):
                self.add(self.zat(zb, lax.rem(at.z + d, 8)), rx3.at[d - 1], at.zp[d - 1])
            self.total(rx3, at.zp[0])
        elif k == 4:
            acc = self.zat(zb, at.z)[...]
            for d in range(7):
                acc = acc + rx3[d]
            mine = self.zat(zo, at.z)
            mine[...] = acc
            for d in range(1, 8):
                self.add(mine, mine, at.zp[d - 1])
            self.total(rx3, at.zp[0])
        elif k == 5:
            o[pl.ds(m8(h0 + a1), F), :] = zo[0:F, :]
            o[pl.ds(m8(h0 + b1), F), :] = zo[F : 2 * F, :]
            ra, rb = o.at[pl.ds(m8(h0 + a1), F)], o.at[pl.ds(m8(h0 + b1), F)]
            for d in range(1, 4):
                self.add(ra, ra, at.yp[d - 1])
                self.add(rb, rb, at.xp[d - 1])
            self.total(rx2, at.xp[0])
        elif k == 6:
            ra, rb = o.at[pl.ds(m8(h0 + a0), E)], o.at[pl.ds(m8(h0 + b0), E)]
            for d in range(1, 4):
                self.add(ra, ra, at.xp[d - 1])
                self.add(rb, rb, at.yp[d - 1])
            self.total(rx1, at.xp[0])
        elif k == 7:
            half = o.at[pl.ds(h0, H)]
            self.add(half, half, at.core)
            self.total(rx0, at.core)


class MidSum(Stage):
    def __init__(self, n, at, src, o, bufs, ss, rs):
        super().__init__(ss, rs)
        self.n, self.at, self.src, self.o = n, at, src, o
        self.gref, self.rx0, self.rx1, self.rx2 = bufs
        self.r = n // 16

    def lanes(self, ref, c):
        return ref.at[:, pl.ds(pl.multiple_of(c * 128, 128), 128)]

    def step(self):
        at, r, gref, rx0, rx1, rx2 = self.at, self.r, self.gref, self.rx0, self.rx1, self.rx2
        k = self.begin()
        own = m8((at.x * 4 + at.y) * r)
        if k == 0:
            self.add(self.lanes(self.src, 1 - at.c), rx0, at.core)
            self.total(rx0, at.core)
        elif k == 1:
            gref[...] = self.lanes(self.src, at.c)[...] + rx0[...]
            for d in range(1, 16):
                to = lax.rem(at.x + d // 4, 4) * 4 + lax.rem(at.y + d % 4, 4)
                self.add(gref.at[pl.ds(m8(to * r), r)], rx1.at[d - 1], at.xyp[d - 1])
            self.total(rx1, at.xyp[0])
        elif k == 2:
            acc = gref[pl.ds(own, r), :]
            for d in range(15):
                acc = acc + rx1[d]
            rx2[at.z] = acc
            mine = rx2.at[at.z]
            for d in range(7):
                self.add(mine, mine, at.zp[d])
            self.total(rx2.at[pl.ds(0, 7)], at.zp[0])
        elif k == 3:
            acc = rx2[0]
            for d in range(1, 8):
                acc = acc + rx2[d]
            mine = self.o.at[pl.ds(own, r), pl.ds(pl.multiple_of(at.c * 128, 128), 128)]
            mine[...] = acc
            for d in range(15):
                self.add(mine, mine, at.xyp[d])
            self.total(rx1, at.xyp[0])
        elif k == 4:
            half = self.lanes(self.o, at.c)
            self.add(half, half, at.core)
            self.total(rx0, at.core)


def mid_scratch(n):
    r = n // 16
    return [
        pltpu.VMEM((n, 256), f32),
        pltpu.VMEM((n, 128), f32),
        pltpu.VMEM((n, 128), f32),
        pltpu.VMEM((15, r, 128), f32),
        pltpu.VMEM((8, r, 128), f32),
        pltpu.SemaphoreType.DMA((5,)),
        pltpu.SemaphoreType.DMA((5,)),
    ]


def small_scratch(r):
    return [
        pltpu.VMEM((8, r, 128), f32),
        pltpu.VMEM((8, r, 128), f32),
        pltpu.VMEM((7, r, 128), f32),
        pltpu.VMEM((8, r, 128), f32),
        pltpu.SemaphoreType.DMA((3,)),
        pltpu.SemaphoreType.DMA((3,)),
    ]


def big_scratch(n):
    H, E, F = n // 2, n // 16, n // 64
    return [
        pltpu.VMEM((n, 256), f32),
        pltpu.VMEM((H, 256), f32),
        pltpu.VMEM((H, 256), f32),
        pltpu.VMEM((2, 3, E, 256), f32),
        pltpu.VMEM((2, 3, F, 256), f32),
        pltpu.VMEM((7, F // 2, 128), f32),
        pltpu.VMEM((2 * F, 256), f32),
        pltpu.VMEM((2 * F, 256), f32),
        pltpu.SemaphoreType.DMA((8,)),
        pltpu.SemaphoreType.DMA((8,)),
    ]


def dg(a, b, ca, cb, precision=None):
    return lax.dot_general(a, b, (((ca,), (cb,)), ((), ())), preferred_element_type=f32, precision=precision)


def exact(a, b, ca, cb):
    return dg(a, b, ca, cb, HIGHEST)


def split(v):
    hi = v.astype(bf16)
    return hi, (v - hi.astype(f32)).astype(bf16)


def iota(shape, dim):
    return lax.broadcasted_iota(jnp.int32, shape, dim)


def block_sum(v, ones):
    out = []
    for half in range(2):
        hi, lo = split(v[:, half * 256 : (half + 1) * 256])
        out.append(dg(hi, ones, 1, 0) + dg(lo, ones, 1, 0))
    return jnp.concatenate(out, axis=1)


def spread_heads(t):
    lanes = iota((HEAD_DIM, HM), 1) // SLICES
    return jnp.concatenate([jnp.where(lanes == h, t, 0.0) for h in range(HEADS)], axis=0)


def gather_heads(ref):
    lanes = iota((HEAD_DIM, HM), 1) // SLICES
    acc = jnp.zeros((HEAD_DIM, HM), f32)
    for h in range(HEADS):
        acc = jnp.where(lanes == h, ref[h * HEAD_DIM : (h + 1) * HEAD_DIM, :], acc)
    return acc


def mean_rows(v):
    return jnp.sum(v, axis=1, keepdims=True) * (1.0 / D)


def norm_parts(v):
    centred = v - mean_rows(v)
    rstd = lax.rsqrt(mean_rows(centred * centred) + EPS)
    return centred * rstd, rstd


def norm_back(dn, xhat, rstd, gain):
    dxh = dn * gain
    return rstd * (dxh - mean_rows(dxh) - xhat * mean_rows(dxh * xhat))


def fold8(v):
    return jnp.sum(v.reshape(v.shape[0] // 8, 8, v.shape[1]), axis=0)


def main_kernel(
    temp_ref, *rest,
):
    hbm, outs, bufs, load_sem, rest = rest[:13], rest[13:17], rest[17:30], rest[30], rest[31:]
    x_ref, dy_ref, gain1_ref, wmid_ref, wfeat_ref, ws_ref, wq_ref, wk_ref, wv_ref, wout_ref, gain2_ref, wup_ref, wdown_ref = bufs
    (
    cells_ref, o1_ref, o2_ref, o3_ref,
    ) = outs
    (
    l_ref, w_ref, du_ref, dh_ref, normed1t_ref, midt_ref, dstate_ref, dw2_ref, bds_ref, bdm_ref, bdw_ref, p_ref,
    s1, so1, s1a, s1b, ss1, rs1, s2, so2, s2a, s2b, ss2, rs2,
    g1, g1a, g1b, g1c, g1d, g1e, g1f, g1g, ss3, rs3, g2, g2a, g2b, g2c, g2d, ss4, rs4,
    g3, g3a, g3b, g3c, g3d, ss5, rs5,
    ) = rest
    loads = [pltpu.make_async_copy(hbm[i], bufs[i], load_sem.at[i]) for i in range(13)]
    for i in (0, 3, 4, 2, 5, 6, 7, 8, 9, 10, 1, 11, 12):
        loads[i].start()
    at = Place()
    everyone = at.everyone
    sem = pltpu.get_barrier_semaphore()
    for dev in everyone:
        pl.semaphore_signal(sem, inc=1, device_id=dev, device_id_type=MESH)
    sum1 = SmallSum(at, s1, so1, s1a, s1b, ss1, rs1)
    sum2 = SmallSum(at, s2, so2, s2a, s2b, ss2, rs2)
    big1 = BigSum(N1, at, g1, o1_ref, (g1a, g1b, g1c, g1d, g1e, g1f, g1g), ss3, rs3)
    mid2 = MidSum(N2, at, g2, o2_ref, (g2a, g2b, g2c, g2d), ss4, rs4)
    tail = MidSum(N3, at, g3, o3_ref, (g3a, g3b, g3c, g3d), ss5, rs5)

    for i in (0, 3, 4, 2, 5):
        loads[i].wait()

    head_of_lane = iota((1, HM), 1) // SLICES
    temp = jnp.zeros((1, HM), f32)
    for h in range(HEADS):
        temp = jnp.where(head_of_lane == h, temp_ref[h], temp)
    inv_temp = 1.0 / temp
    ones = (iota((256, 256), 0) // SLICES == iota((256, 256), 1) // SLICES).astype(f32).astype(bf16)
    place = (iota((SLICES, HM), 0) == lax.rem(iota((SLICES, HM), 1), SLICES)).astype(f32)
    wide = dg(ws_ref[...], place.astype(bf16), 1, 0)
    bds_ref[...] = spread_heads(wide).astype(bf16)
    gain1 = gain1_ref[...]

    xhat1, rstd1 = norm_parts(x_ref[...].astype(f32))
    normed1 = (xhat1 * gain1).astype(bf16)
    mid = dg(normed1, wmid_ref[...], 1, 0)
    feat = dg(normed1, wfeat_ref[...], 1, 0).astype(bf16)
    mid_hi, mid_lo = split(mid)
    logits = (dg(mid_hi, bds_ref[...], 1, 0) + dg(mid_lo, bds_ref[...], 1, 0)) * inv_temp
    l_ref[...] = logits
    e = jnp.exp(logits)
    w = e / block_sum(e, ones)
    w_ref[...] = w
    wb = w.astype(bf16)
    tt = gather_heads(dg(feat, wb, 0, 0))
    tot = fold8(w)
    for j in range(8):
        lanes = slice((j // 2) * 128, (j // 2 + 1) * 128)
        s1[j, 0:16, :] = tt[(j % 2) * 16 : (j % 2 + 1) * 16, lanes]
        s1[j, 16:24, :] = tot[:, lanes]

    pl.semaphore_wait(sem, len(everyone))
    sum1.step()
    for i in (1, 12):
        loads[i].wait()
    dy = dy_ref[...]
    for j in range(2):
        cols = slice(j * 256, (j + 1) * 256)
        dh_ref[:, cols] = dg(dy, wdown_ref[cols, :], 1, 1).astype(bf16)
    sum1.step()
    for j in range(2, 4):
        cols = slice(j * 256, (j + 1) * 256)
        dh_ref[:, cols] = dg(dy, wdown_ref[cols, :], 1, 1).astype(bf16)
    sum1.step()
    normed1t_ref[...] = normed1.T
    midt_ref[...] = mid_hi.T
    for i in (6, 7, 8, 9, 10, 11):
        loads[i].wait()
    gain2 = gain2_ref[...]
    sum1.wait()

    wq, wk, wv = (r[...].astype(f32) for r in (wq_ref, wk_ref, wv_ref))
    scale = HEAD_DIM**-0.5
    same = iota((128, 128), 0) // SLICES == iota((128, 128), 1) // SLICES
    mix = []
    kept = []
    for b in range(4):
        total = jnp.sum(so1[2 * b, 16:24, :], axis=0, keepdims=True)
        tok = jnp.concatenate([so1[2 * b, 0:16, :], so1[2 * b + 1, 0:16, :]], axis=0) / total
        q = exact(wq, tok, 0, 0)
        k = exact(wk, tok, 0, 0)
        v = exact(wv, tok, 0, 0)
        sc = exact(q, k, 0, 0) * scale
        e = jnp.where(same, jnp.exp(jnp.where(same, sc, 0.0)), 0.0)
        prob = e / jnp.sum(e, axis=1, keepdims=True)
        p_ref[b] = prob
        mix.append(exact(v, prob, 1, 1))
        kept.append((total, tok, q, k, v))
    hi, lo = split(spread_heads(jnp.concatenate(mix, axis=1)))
    bdm_ref[0] = hi
    bdm_ref[1] = lo

    sp = (dg(wb, bdm_ref[0], 1, 1) + dg(wb, bdm_ref[1], 1, 1)).astype(bf16)
    state = x_ref[...].astype(f32) + dg(sp, wout_ref[...], 1, 0)
    xhat2, rstd2 = norm_parts(state)
    normed2 = (xhat2 * gain2).astype(bf16)
    normed2t = normed2.T
    dy = dy_ref[...]
    for j in range(4):
        cols = slice(j * 256, (j + 1) * 256)
        u = dg(normed2, wup_ref[:, cols], 1, 0)
        u2 = u * u
        t = jnp.tanh(u * (GELU_C + (GELU_C * GELU_A) * u2))
        half = 0.5 + 0.5 * t
        hidden = (u * half).astype(bf16)
        slope = half + u * half * (1.0 - t) * (GELU_C + (3.0 * GELU_C * GELU_A) * u2)
        du = (dh_ref[:, cols].astype(f32) * slope).astype(bf16)
        du_ref[:, cols] = du
        g1[j * 256 : (j + 1) * 256, :] = dg(hidden, dy, 0, 0)
        g1[1024 + j * 256 : 1280 + j * 256, :] = dg(normed2t, du, 1, 0)
    dn = dg(du_ref[...], wup_ref[...], 1, 1).astype(bf16).astype(f32)
    g_gain2 = jnp.sum(dn * xhat2, axis=0, keepdims=True)
    ds = dy.astype(f32) + norm_back(dn, xhat2, rstd2, gain2)
    dstate_ref[...] = ds
    dsb = ds.astype(bf16)
    dsp = dg(dsb, wout_ref[...], 1, 1).astype(bf16)
    dmt = gather_heads(dg(dsp, wb, 0, 0))
    for j in range(8):
        s2[j] = dmt[(j % 2) * 16 : (j % 2 + 1) * 16, (j // 2) * 128 : (j // 2 + 1) * 128]
    sum2.step()
    big1.step()
    dw2_ref[...] = dg(dsp, bdm_ref[0], 1, 0) + dg(dsp, bdm_ref[1], 1, 0)
    sum2.step()
    big1.step()
    g2[0:256, :] = dg(sp, dsb, 0, 0)
    sum2.step()
    sum2.wait()

    gq = jnp.zeros((HEAD_DIM, HEAD_DIM), f32)
    gk, gv = gq, gq
    dwt, dtot = [], []
    for b in range(4):
        total, tok, q, k, v = kept[b]
        prob = p_ref[b]
        dm = jnp.concatenate([so2[2 * b], so2[2 * b + 1]], axis=0)
        dp = exact(dm, v, 0, 0)
        dsc = prob * (dp - jnp.sum(prob * dp, axis=1, keepdims=True)) * scale
        dq = exact(k, dsc, 1, 1)
        dk = exact(q, dsc, 1, 0)
        dv = exact(dm, prob, 1, 0)
        gq = gq + exact(tok, dq, 1, 1)
        gk = gk + exact(tok, dk, 1, 1)
        gv = gv + exact(tok, dv, 1, 1)
        dtok = exact(wq, dq, 1, 0) + exact(wk, dk, 1, 0) + exact(wv, dv, 1, 0)
        dtok = dtok / total
        dwt.append(dtok)
        dtot.append(-jnp.sum(dtok * tok, axis=0, keepdims=True))
    hi, lo = split(spread_heads(jnp.concatenate(dwt, axis=1)))
    bdw_ref[0] = hi
    bdw_ref[1] = lo
    d_totals = jnp.concatenate(dtot, axis=1)

    dfeat = (dg(wb, bdw_ref[0], 1, 1) + dg(wb, bdw_ref[1], 1, 1)).astype(bf16)
    g2[256:512, :] = dg(normed1t_ref[...], dfeat, 1, 0)
    mid2.step()
    dw = dw2_ref[...] + dg(feat, bdw_ref[0], 1, 0) + dg(feat, bdw_ref[1], 1, 0) + d_totals
    w = w_ref[...]
    dl = w * (dw - block_sum(w * dw, ones))
    dlt = (dl * inv_temp).astype(bf16)
    dmid = dg(dlt, bds_ref[...], 1, 1).astype(bf16)
    g3[0:256, :] = dg(normed1t_ref[...], dmid, 1, 0)
    big1.step()
    dn = dg(dmid, wmid_ref[...], 1, 1).astype(bf16).astype(f32) + dg(dfeat, wfeat_ref[...], 1, 1).astype(bf16).astype(
        f32
    )
    dn = dn.astype(bf16).astype(f32)
    xhat1, rstd1 = norm_parts(x_ref[...].astype(f32))

    first = (lax.axis_index("point") == 0).astype(f32)
    g3[SMALL:N3, :] = jnp.zeros((N3 - SMALL, 256), f32)
    pick = (iota((HM, 256), 0) // SLICES == iota((HM, 256), 1)).astype(f32)
    inv8 = jnp.zeros((1, 256), f32)
    for h in range(HEADS):
        inv8 = jnp.where(iota((1, 256), 1) == h, 1.0 / temp_ref[h], inv8)
    g_temp = jnp.sum(exact(fold8(dl * l_ref[...]), pick, 1, 0), axis=0, keepdims=True) * (-inv8)
    g3[SMALL : SMALL + 1, :] = jnp.sum(dn * xhat1, axis=0, keepdims=True)
    g3[SMALL + 1 : SMALL + 2, :] = g_gain2
    g3[SMALL + 2 : SMALL + 3, :] = g_temp
    g3[SMALL + 8 : SMALL + 40, 0:64] = exact(gather_heads(dg(midt_ref[...], dlt, 1, 0)), place, 1, 1)
    g3[SMALL + 8 : SMALL + 40, 128:160] = gq * first
    g3[SMALL + 40 : SMALL + 72, 0:32] = gk * first
    g3[SMALL + 40 : SMALL + 72, 128:160] = gv * first
    tail.step()
    mid2.step()
    big1.step()
    cells_ref[...] = (norm_back(dn, xhat1, rstd1, gain1) + dstate_ref[...]).astype(bf16)
    tail.step()
    big1.step()
    mid2.step()
    tail.step()
    big1.step()
    mid2.step()
    tail.step()
    big1.step()
    mid2.step()
    tail.step()
    big1.step()
    mid2.step()
    tail.step()
    mid2.step()
    big1.step()


def out_kernel(
    hbm_cells, hbm1, hbm2, hbm3,
    cells_out, gain1, mid, feat, slc, temp, wq, wk, wv, wout, gain2, up, down,
    o1, o3, sems,
):
    pairs = ((hbm1, o1), (hbm3, o3), (hbm_cells, cells_out), (hbm2.at[0:256, :], wout), (hbm2.at[256:512, :], feat))
    copies = [pltpu.make_async_copy(a, b, sems.at[i]) for i, (a, b) in enumerate(pairs)]
    for cp in copies:
        cp.start()
    copies[1].wait()
    mid[...] = o3[0:256, :]
    gain1[...] = o3[SMALL : SMALL + 1, :]
    gain2[...] = o3[SMALL + 1 : SMALL + 2, :]
    temp[...] = o3[SMALL + 2 : SMALL + 3, 0:8]
    slc[...] = o3[SMALL + 8 : SMALL + 40, 0:64]
    wq[...] = o3[SMALL + 8 : SMALL + 40, 128:160]
    wk[...] = o3[SMALL + 40 : SMALL + 72, 0:32]
    wv[...] = o3[SMALL + 40 : SMALL + 72, 128:160]
    copies[0].wait()
    down[...] = o1[0:1024, :]
    for j in range(4):
        up[:, j * 256 : (j + 1) * 256] = o1[1024 + j * 256 : 1280 + j * 256, :]
    for cp in copies[2:]:
        cp.wait()


vmem_ = pl.BlockSpec(memory_space=pltpu.VMEM)
any_ = pl.BlockSpec(memory_space=pl.ANY)


def vmem(count):
    return [vmem_] * count


def anys(count):
    return [any_] * count


def on_device(x, dy, gain1, wmid, wfeat, ws, temp, wq, wk, wv, wout, gain2, wup, wdown):
    sds = jax.ShapeDtypeStruct
    operands = (
        x[0], dy[0], gain1.reshape(1, D), wmid, wfeat, ws, wq, wk, wv, wout, gain2.reshape(1, D), wup, wdown,
    )
    cells, o1, o2, o3 = pl.pallas_call(
        main_kernel,
        out_shape=(sds((CELLS, D), bf16), sds((N1, 256), f32), sds((N2, 256), f32), sds((N3, 256), f32)),
        in_specs=[pl.BlockSpec(memory_space=pltpu.SMEM)] + [pl.BlockSpec(memory_space=pltpu.HBM)] * 13,
        out_specs=vmem(4),
        scratch_shapes=[pltpu.VMEM(a.shape, a.dtype) for a in operands]
        + [
            pltpu.SemaphoreType.DMA((13,)),
            pltpu.VMEM((CELLS, HM), f32),
            pltpu.VMEM((CELLS, HM), f32),
            pltpu.VMEM((CELLS, FF), bf16),
            pltpu.VMEM((CELLS, FF), bf16),
            pltpu.VMEM((D, CELLS), bf16),
            pltpu.VMEM((D, CELLS), bf16),
            pltpu.VMEM((CELLS, D), f32),
            pltpu.VMEM((CELLS, HM), f32),
            pltpu.VMEM((D, HM), bf16),
            pltpu.VMEM((2, D, HM), bf16),
            pltpu.VMEM((2, D, HM), bf16),
            pltpu.VMEM((4, 128, 128), f32),
        ]
        + small_scratch(24)
        + small_scratch(16)
        + big_scratch(N1)
        + mid_scratch(N2)
        + mid_scratch(N3),
        compiler_params=pltpu.CompilerParams(
            collective_id=0, has_side_effects=True, vmem_limit_bytes=56 * 2**20
        ),
    )(temp, *operands)
    outs = pl.pallas_call(
        out_kernel,
        out_shape=(
            sds((CELLS, D), bf16), sds((1, D), f32), sds((D, D), f32), sds((D, D), f32),
            sds((HEAD_DIM, SLICES), f32), sds((1, HEADS), f32), sds((HEAD_DIM, HEAD_DIM), f32),
            sds((HEAD_DIM, HEAD_DIM), f32), sds((HEAD_DIM, HEAD_DIM), f32), sds((D, D), f32), sds((1, D), f32),
            sds((D, FF), f32), sds((FF, D), f32),
        ),
        in_specs=[pl.BlockSpec(memory_space=pltpu.HBM)] * 4,
        out_specs=vmem(13),
        scratch_shapes=[
            pltpu.VMEM((N1, 256), f32),
            pltpu.VMEM((N3, 256), f32),
            pltpu.SemaphoreType.DMA((5,)),
        ],
        compiler_params=pltpu.CompilerParams(vmem_limit_bytes=56 * 2**20),
    )(cells, o1, o2, o3)
    outs = list(outs)
    outs[0] = outs[0][None]
    outs[1] = outs[1].reshape(D)
    outs[5] = outs[5].reshape(HEADS)
    outs[10] = outs[10].reshape(D)
    return tuple(outs)


def solution(mesh):
    return jax.shard_map(
        on_device,
        mesh=mesh,
        in_specs=(P("dp", "point", None), P("dp", "point", None)) + (P(),) * 12,
        out_specs=(P("dp", "point", None),) + (P(),) * 12,
        check_vma=False,
    )
```

```python
import functools
import jax
import jax.numpy as jnp
from jax import lax
from jax.experimental import pallas as pl
from jax.experimental.pallas import tpu as pltpu
from jax.sharding import PartitionSpec as P

MESH = pl.DeviceIdType.MESH
HIGHEST = lax.Precision.HIGHEST
f32 = jnp.float32
bf16 = jnp.bfloat16

CELLS = 768
D = 256
FF = 1024
HEADS = 8
SLICES = 64
HEAD_DIM = 32
HM = HEADS * SLICES
EPS = 1e-05
N1 = 2048
N2 = 512
N3 = 384
SMALL = 256
GELU_C = 0.7978845608028654
GELU_A = 0.044715


def rcopy(src, dst, ss, rs, dev):
    return pltpu.make_async_remote_copy(
        src_ref=src, dst_ref=dst, send_sem=ss, recv_sem=rs, device_id=dev, device_id_type=MESH
    )


def m8(v):
    return pl.multiple_of(v, 8)


class Place:
    def __init__(self):
        self.y = lax.axis_index("dp")
        p = lax.axis_index("point")
        self.z = p // 8
        self.g = lax.rem(p, 8)
        self.x = self.g // 2
        self.c = lax.rem(self.g, 2)
        z, x, c, g, y = self.z, self.x, self.c, self.g, self.y
        self.core = {"point": z * 8 + x * 2 + (1 - c)}
        self.gp = [{"point": z * 8 + lax.rem(g + d, 8)} for d in range(1, 8)]
        self.zp = [{"point": lax.rem(z + d, 8) * 8 + g} for d in range(1, 8)]
        self.xp = [{"point": z * 8 + lax.rem(x + d, 4) * 2 + c} for d in range(1, 4)]
        self.yp = [{"dp": lax.rem(y + d, 4)} for d in range(1, 4)]
        self.xyp = [
            {"dp": lax.rem(y + d % 4, 4), "point": z * 8 + lax.rem(x + d // 4, 4) * 2 + c} for d in range(1, 16)
        ]
        far = [self.xyp[d - 1] for d in range(1, 16) if d % 4]
        self.everyone = self.gp + self.zp + far


class Stage:
    def __init__(self, ss, rs):
        self.ss, self.rs, self.k, self.pending = ss, rs, -1, None
        self.copies = []

    def wait(self):
        if self.pending is not None:
            self.pending.wait_send()
            self.pending.wait_recv()
        self.pending = None
        self.copies = []

    def begin(self):
        self.wait()
        self.k += 1
        return self.k

    def add(self, src, dst, dev):
        rcopy(src, dst, self.ss.at[self.k], self.rs.at[self.k], dev).start()

    def total(self, ref, dev):
        self.pending = rcopy(ref, ref, self.ss.at[self.k], self.rs.at[self.k], dev)


class SmallSum(Stage):
    def __init__(self, at, s, o, rx1, rx2, ss, rs):
        super().__init__(ss, rs)
        self.at, self.s, self.o, self.rx1, self.rx2 = at, s, o, rx1, rx2

    def step(self):
        at, s, o, rx1, rx2 = self.at, self.s, self.o, self.rx1, self.rx2
        k = self.begin()
        if k == 0:
            for d in range(1, 8):
                self.add(s.at[lax.rem(at.g + d, 8)], rx1.at[d - 1], at.gp[d - 1])
            self.total(rx1, at.gp[0])
        elif k == 1:
            acc = s[at.g]
            for d in range(7):
                acc = acc + rx1[d]
            rx2[at.z] = acc
            mine = rx2.at[at.z]
            for d in range(7):
                self.add(mine, mine, at.zp[d])
            self.total(rx1, at.zp[0])
        elif k == 2:
            acc = rx2[0]
            for d in range(1, 8):
                acc = acc + rx2[d]
            o[at.g] = acc
            mine = o.at[at.g]
            for d in range(7):
                self.add(mine, mine, at.gp[d])
            self.total(rx1, at.gp[0])


def add_rows(dst, d0, base, b0, srcs, rows):
    t = min(rows, 64)

    def body(i, _):
        o = pl.multiple_of(i * t, t)
        acc = base[pl.ds(m8(b0 + o), t), :]
        for s in srcs:
            acc = acc + s[pl.ds(o, t), :]
        dst[pl.ds(m8(d0 + o), t), :] = acc
        return 0

    lax.fori_loop(0, rows // t, body, 0)


class BigSum(Stage):
    def __init__(self, n, at, src, o, bufs, ss, rs):
        super().__init__(ss, rs)
        self.n, self.at, self.src, self.o = n, at, src, o
        self.gref, self.rx0, self.rx1, self.rx2, self.rx3, self.zb, self.zo = bufs
        self.H, self.Q, self.E, self.F = n // 2, n // 4, n // 16, n // 64
        self.K = self.F // 2
        E, F, Q, H = self.E, self.F, self.Q, self.H
        self.h0 = m8(at.c * H)
        self.a0, self.b0 = m8(at.x * E), m8(Q + at.y * E)
        self.a1, self.b1 = m8(self.a0 + at.y * F), m8(self.b0 + at.x * F)

    def zat(self, ref, k):
        K = self.K
        return ref.at[pl.ds(m8((k // 2) * K), K), pl.ds(pl.multiple_of(lax.rem(k, 2) * 128, 128), 128)]

    def step(self):
        at, H, Q, E, F = self.at, self.H, self.Q, self.E, self.F
        gref, rx0, rx1, rx2, rx3, zb, zo, o = (
            self.gref, self.rx0, self.rx1, self.rx2, self.rx3, self.zb, self.zo, self.o,
        )
        h0, a0, b0, a1, b1 = self.h0, self.a0, self.b0, self.a1, self.b1
        k = self.begin()
        if k == 0:
            self.add(self.src.at[pl.ds(m8((1 - at.c) * H), H)], rx0, at.core)
            self.total(rx0, at.core)
        elif k == 1:
            add_rows(gref, 0, self.src, h0, [rx0], H)
            for d in range(1, 4):
                xi, yi = lax.rem(at.x + d, 4), lax.rem(at.y + d, 4)
                self.add(gref.at[pl.ds(m8(xi * E), E)], rx1.at[0, d - 1], at.xp[d - 1])
                self.add(gref.at[pl.ds(m8(Q + yi * E), E)], rx1.at[1, d - 1], at.yp[d - 1])
            self.total(rx1, at.xp[0])
        elif k == 2:
            add_rows(gref, a0, gref, a0, [rx1.at[0, d] for d in range(3)], E)
            add_rows(gref, b0, gref, b0, [rx1.at[1, d] for d in range(3)], E)
            for d in range(1, 4):
                xi, yi = lax.rem(at.x + d, 4), lax.rem(at.y + d, 4)
                self.add(gref.at[pl.ds(m8(a0 + yi * F), F)], rx2.at[0, d - 1], at.yp[d - 1])
                self.add(gref.at[pl.ds(m8(b0 + xi * F), F)], rx2.at[1, d - 1], at.xp[d - 1])
            self.total(rx2, at.xp[0])
        elif k == 3:
            add_rows(zb, 0, gref, a1, [rx2.at[0, d] for d in range(3)], F)
            add_rows(zb, F, gref, b1, [rx2.at[1, d] for d in range(3)], F)
            for d in range(1, 8):
                self.add(self.zat(zb, lax.rem(at.z + d, 8)), rx3.at[d - 1], at.zp[d - 1])
            self.total(rx3, at.zp[0])
        elif k == 4:
            acc = self.zat(zb, at.z)[...]
            for d in range(7):
                acc = acc + rx3[d]
            mine = self.zat(zo, at.z)
            mine[...] = acc
            for d in range(1, 8):
                self.add(mine, mine, at.zp[d - 1])
            self.total(rx3, at.zp[0])
        elif k == 5:
            o[pl.ds(m8(h0 + a1), F), :] = zo[0:F, :]
            o[pl.ds(m8(h0 + b1), F), :] = zo[F : 2 * F, :]
            ra, rb = o.at[pl.ds(m8(h0 + a1), F)], o.at[pl.ds(m8(h0 + b1), F)]
            for d in range(1, 4):
                self.add(ra, ra, at.yp[d - 1])
                self.add(rb, rb, at.xp[d - 1])
            self.total(rx2, at.xp[0])
        elif k == 6:
            ra, rb = o.at[pl.ds(m8(h0 + a0), E)], o.at[pl.ds(m8(h0 + b0), E)]
            for d in range(1, 4):
                self.add(ra, ra, at.xp[d - 1])
                self.add(rb, rb, at.yp[d - 1])
            self.total(rx1, at.xp[0])
        elif k == 7:
            half = o.at[pl.ds(h0, H)]
            self.add(half, half, at.core)
            self.total(rx0, at.core)


class MidSum(Stage):
    def __init__(self, n, at, src, o, bufs, ss, rs):
        super().__init__(ss, rs)
        self.n, self.at, self.src, self.o = n, at, src, o
        self.gref, self.rx0, self.rx1, self.rx2 = bufs
        self.r = n // 16

    def lanes(self, ref, c):
        return ref.at[:, pl.ds(pl.multiple_of(c * 128, 128), 128)]

    def step(self):
        at, r, gref, rx0, rx1, rx2 = self.at, self.r, self.gref, self.rx0, self.rx1, self.rx2
        k = self.begin()
        own = m8((at.x * 4 + at.y) * r)
        if k == 0:
            self.add(self.lanes(self.src, 1 - at.c), rx0, at.core)
            self.total(rx0, at.core)
        elif k == 1:
            gref[...] = self.lanes(self.src, at.c)[...] + rx0[...]
            for d in range(1, 16):
                to = lax.rem(at.x + d // 4, 4) * 4 + lax.rem(at.y + d % 4, 4)
                self.add(gref.at[pl.ds(m8(to * r), r)], rx1.at[d - 1], at.xyp[d - 1])
            self.total(rx1, at.xyp[0])
        elif k == 2:
            acc = gref[pl.ds(own, r), :]
            for d in range(15):
                acc = acc + rx1[d]
            rx2[at.z] = acc
            mine = rx2.at[at.z]
            for d in range(7):
                self.add(mine, mine, at.zp[d])
            self.total(rx2.at[pl.ds(0, 7)], at.zp[0])
        elif k == 3:
            acc = rx2[0]
            for d in range(1, 8):
                acc = acc + rx2[d]
            mine = self.o.at[pl.ds(own, r), pl.ds(pl.multiple_of(at.c * 128, 128), 128)]
            mine[...] = acc
            for d in range(15):
                self.add(mine, mine, at.xyp[d])
            self.total(rx1, at.xyp[0])
        elif k == 4:
            half = self.lanes(self.o, at.c)
            self.add(half, half, at.core)
            self.total(rx0, at.core)


def mid_scratch(n):
    r = n // 16
    return [
        pltpu.VMEM((n, 256), f32),
        pltpu.VMEM((n, 128), f32),
        pltpu.VMEM((n, 128), f32),
        pltpu.VMEM((15, r, 128), f32),
        pltpu.VMEM((8, r, 128), f32),
        pltpu.SemaphoreType.DMA((5,)),
        pltpu.SemaphoreType.DMA((5,)),
    ]


def small_scratch(r):
    return [
        pltpu.VMEM((8, r, 128), f32),
        pltpu.VMEM((8, r, 128), f32),
        pltpu.VMEM((7, r, 128), f32),
        pltpu.VMEM((8, r, 128), f32),
        pltpu.SemaphoreType.DMA((3,)),
        pltpu.SemaphoreType.DMA((3,)),
    ]


def big_scratch(n):
    H, E, F = n // 2, n // 16, n // 64
    return [
        pltpu.VMEM((n, 256), f32),
        pltpu.VMEM((H, 256), f32),
        pltpu.VMEM((H, 256), f32),
        pltpu.VMEM((2, 3, E, 256), f32),
        pltpu.VMEM((2, 3, F, 256), f32),
        pltpu.VMEM((7, F // 2, 128), f32),
        pltpu.VMEM((2 * F, 256), f32),
        pltpu.VMEM((2 * F, 256), f32),
        pltpu.SemaphoreType.DMA((8,)),
        pltpu.SemaphoreType.DMA((8,)),
    ]


def dg(a, b, ca, cb, precision=None):
    return lax.dot_general(a, b, (((ca,), (cb,)), ((), ())), preferred_element_type=f32, precision=precision)


def exact(a, b, ca, cb):
    return dg(a, b, ca, cb, HIGHEST)


def split(v):
    hi = v.astype(bf16)
    return hi, (v - hi.astype(f32)).astype(bf16)


def iota(shape, dim):
    return lax.broadcasted_iota(jnp.int32, shape, dim)


def block_sum(v, ones):
    out = []
    for half in range(2):
        hi, lo = split(v[:, half * 256 : (half + 1) * 256])
        out.append(dg(hi, ones, 1, 0) + dg(lo, ones, 1, 0))
    return jnp.concatenate(out, axis=1)


def spread_heads(t):
    lanes = iota((HEAD_DIM, HM), 1) // SLICES
    return jnp.concatenate([jnp.where(lanes == h, t, 0.0) for h in range(HEADS)], axis=0)


def gather_heads(ref):
    lanes = iota((HEAD_DIM, HM), 1) // SLICES
    acc = jnp.zeros((HEAD_DIM, HM), f32)
    for h in range(HEADS):
        acc = jnp.where(lanes == h, ref[h * HEAD_DIM : (h + 1) * HEAD_DIM, :], acc)
    return acc


def mean_rows(v):
    return jnp.sum(v, axis=1, keepdims=True) * (1.0 / D)


def norm_parts(v):
    centred = v - mean_rows(v)
    rstd = lax.rsqrt(mean_rows(centred * centred) + EPS)
    return centred * rstd, rstd


def norm_back(dn, xhat, rstd, gain):
    dxh = dn * gain
    return rstd * (dxh - mean_rows(dxh) - xhat * mean_rows(dxh * xhat))


def fold8(v):
    return jnp.sum(v.reshape(v.shape[0] // 8, 8, v.shape[1]), axis=0)


def main_kernel(
    temp_ref, *rest,
):
    hbm, outs, bufs, load_sem, rest = rest[:13], rest[13:17], rest[17:30], rest[30], rest[31:]
    results, store_sem, rest = rest[:4], rest[4], rest[5:]
    x_ref, dy_ref, gain1_ref, wmid_ref, wfeat_ref, ws_ref, wq_ref, wk_ref, wv_ref, wout_ref, gain2_ref, wup_ref, wdown_ref = bufs
    (
    cells_ref, o1_ref, o2_ref, o3_ref,
    ) = results
    stores = [pltpu.make_async_copy(results[i], outs[i], store_sem.at[i]) for i in range(4)]
    (
    l_ref, w_ref, du_ref, dh_ref, normed1t_ref, midt_ref, dstate_ref, dw2_ref, bds_ref, bdm_ref, bdw_ref, p_ref,
    s1, so1, s1a, s1b, ss1, rs1, s2, so2, s2a, s2b, ss2, rs2,
    g1, g1a, g1b, g1c, g1d, g1e, g1f, g1g, ss3, rs3, g2, g2a, g2b, g2c, g2d, ss4, rs4,
    g3, g3a, g3b, g3c, g3d, ss5, rs5,
    ) = rest
    loads = [pltpu.make_async_copy(hbm[i], bufs[i], load_sem.at[i]) for i in range(13)]
    for i in (0, 3, 4, 2, 5, 6, 7, 8, 9, 10, 1, 11, 12):
        loads[i].start()
    at = Place()
    everyone = at.everyone
    sem = pltpu.get_barrier_semaphore()
    for dev in everyone:
        pl.semaphore_signal(sem, inc=1, device_id=dev, device_id_type=MESH)
    sum1 = SmallSum(at, s1, so1, s1a, s1b, ss1, rs1)
    sum2 = SmallSum(at, s2, so2, s2a, s2b, ss2, rs2)
    big1 = BigSum(N1, at, g1, o1_ref, (g1a, g1b, g1c, g1d, g1e, g1f, g1g), ss3, rs3)
    mid2 = MidSum(N2, at, g2, o2_ref, (g2a, g2b, g2c, g2d), ss4, rs4)
    tail = MidSum(N3, at, g3, o3_ref, (g3a, g3b, g3c, g3d), ss5, rs5)

    for i in (0, 3, 4, 2, 5):
        loads[i].wait()

    head_of_lane = iota((1, HM), 1) // SLICES
    temp = jnp.zeros((1, HM), f32)
    for h in range(HEADS):
        temp = jnp.where(head_of_lane == h, temp_ref[h], temp)
    inv_temp = 1.0 / temp
    ones = (iota((256, 256), 0) // SLICES == iota((256, 256), 1) // SLICES).astype(f32).astype(bf16)
    place = (iota((SLICES, HM), 0) == lax.rem(iota((SLICES, HM), 1), SLICES)).astype(f32)
    wide = dg(ws_ref[...], place.astype(bf16), 1, 0)
    bds_ref[...] = spread_heads(wide).astype(bf16)
    gain1 = gain1_ref[...]

    xhat1, rstd1 = norm_parts(x_ref[...].astype(f32))
    normed1 = (xhat1 * gain1).astype(bf16)
    mid = dg(normed1, wmid_ref[...], 1, 0)
    feat = dg(normed1, wfeat_ref[...], 1, 0).astype(bf16)
    mid_hi, mid_lo = split(mid)
    logits = (dg(mid_hi, bds_ref[...], 1, 0) + dg(mid_lo, bds_ref[...], 1, 0)) * inv_temp
    l_ref[...] = logits
    e = jnp.exp(logits)
    w = e / block_sum(e, ones)
    w_ref[...] = w
    wb = w.astype(bf16)
    tt = gather_heads(dg(feat, wb, 0, 0))
    tot = fold8(w)
    for j in range(8):
        lanes = slice((j // 2) * 128, (j // 2 + 1) * 128)
        s1[j, 0:16, :] = tt[(j % 2) * 16 : (j % 2 + 1) * 16, lanes]
        s1[j, 16:24, :] = tot[:, lanes]

    pl.semaphore_wait(sem, len(everyone))
    sum1.step()
    for i in (1, 12):
        loads[i].wait()
    dy = dy_ref[...]
    for j in range(2):
        cols = slice(j * 256, (j + 1) * 256)
        dh_ref[:, cols] = dg(dy, wdown_ref[cols, :], 1, 1).astype(bf16)
    sum1.step()
    for j in range(2, 4):
        cols = slice(j * 256, (j + 1) * 256)
        dh_ref[:, cols] = dg(dy, wdown_ref[cols, :], 1, 1).astype(bf16)
    sum1.step()
    normed1t_ref[...] = normed1.T
    midt_ref[...] = mid_hi.T
    for i in (6, 7, 8, 9, 10, 11):
        loads[i].wait()
    gain2 = gain2_ref[...]
    sum1.wait()

    wq, wk, wv = (r[...].astype(f32) for r in (wq_ref, wk_ref, wv_ref))
    scale = HEAD_DIM**-0.5
    same = iota((128, 128), 0) // SLICES == iota((128, 128), 1) // SLICES
    mix = []
    kept = []
    for b in range(4):
        total = jnp.sum(so1[2 * b, 16:24, :], axis=0, keepdims=True)
        tok = jnp.concatenate([so1[2 * b, 0:16, :], so1[2 * b + 1, 0:16, :]], axis=0) / total
        q = exact(wq, tok, 0, 0)
        k = exact(wk, tok, 0, 0)
        v = exact(wv, tok, 0, 0)
        sc = exact(q, k, 0, 0) * scale
        e = jnp.where(same, jnp.exp(jnp.where(same, sc, 0.0)), 0.0)
        prob = e / jnp.sum(e, axis=1, keepdims=True)
        p_ref[b] = prob
        mix.append(exact(v, prob, 1, 1))
        kept.append((total, tok, q, k, v))
    hi, lo = split(spread_heads(jnp.concatenate(mix, axis=1)))
    bdm_ref[0] = hi
    bdm_ref[1] = lo

    sp = dg(wb, bdm_ref[0], 1, 1).astype(bf16)
    state = x_ref[...].astype(f32) + dg(sp, wout_ref[...], 1, 0)
    xhat2, rstd2 = norm_parts(state)
    normed2 = (xhat2 * gain2).astype(bf16)
    normed2t = normed2.T
    dy = dy_ref[...]
    for j in range(4):
        cols = slice(j * 256, (j + 1) * 256)
        u = dg(normed2, wup_ref[:, cols], 1, 0)
        u2 = u * u
        t = jnp.tanh(u * (GELU_C + (GELU_C * GELU_A) * u2))
        half = 0.5 + 0.5 * t
        hidden = (u * half).astype(bf16)
        slope = half + u * half * (1.0 - t) * (GELU_C + (3.0 * GELU_C * GELU_A) * u2)
        du = (dh_ref[:, cols].astype(f32) * slope).astype(bf16)
        du_ref[:, cols] = du
        g1[j * 256 : (j + 1) * 256, :] = dg(hidden, dy, 0, 0)
        g1[1024 + j * 256 : 1280 + j * 256, :] = dg(normed2t, du, 1, 0)
    dn = dg(du_ref[...], wup_ref[...], 1, 1).astype(bf16).astype(f32)
    g_gain2 = jnp.sum(dn * xhat2, axis=0, keepdims=True)
    ds = dy.astype(f32) + norm_back(dn, xhat2, rstd2, gain2)
    dstate_ref[...] = ds
    dsb = ds.astype(bf16)
    dsp = dg(dsb, wout_ref[...], 1, 1).astype(bf16)
    dmt = gather_heads(dg(dsp, wb, 0, 0))
    for j in range(8):
        s2[j] = dmt[(j % 2) * 16 : (j % 2 + 1) * 16, (j // 2) * 128 : (j // 2 + 1) * 128]
    sum2.step()
    big1.step()
    dw2_ref[...] = dg(dsp, bdm_ref[0], 1, 0) + dg(dsp, bdm_ref[1], 1, 0)
    sum2.step()
    big1.step()
    g2[0:256, :] = dg(sp, dsb, 0, 0)
    sum2.step()
    sum2.wait()

    big1.step()
    gq = jnp.zeros((HEAD_DIM, HEAD_DIM), f32)
    gk, gv = gq, gq
    dwt, dtot = [], []
    for b in range(4):
        total, tok, q, k, v = kept[b]
        prob = p_ref[b]
        dm = jnp.concatenate([so2[2 * b], so2[2 * b + 1]], axis=0)
        dp = exact(dm, v, 0, 0)
        dsc = prob * (dp - jnp.sum(prob * dp, axis=1, keepdims=True)) * scale
        dq = exact(k, dsc, 1, 1)
        dk = exact(q, dsc, 1, 0)
        dv = exact(dm, prob, 1, 0)
        gq = gq + exact(tok, dq, 1, 1)
        gk = gk + exact(tok, dk, 1, 1)
        gv = gv + exact(tok, dv, 1, 1)
        dtok = exact(wq, dq, 1, 0) + exact(wk, dk, 1, 0) + exact(wv, dv, 1, 0)
        dtok = dtok / total
        dwt.append(dtok)
        dtot.append(-jnp.sum(dtok * tok, axis=0, keepdims=True))
    hi, lo = split(spread_heads(jnp.concatenate(dwt, axis=1)))
    bdw_ref[0] = hi
    bdw_ref[1] = lo
    d_totals = jnp.concatenate(dtot, axis=1)

    dfeat = dg(wb, bdw_ref[0], 1, 1).astype(bf16)
    g2[256:512, :] = dg(normed1t_ref[...], dfeat, 1, 0)
    mid2.step()
    dw = dw2_ref[...] + dg(feat, bdw_ref[0], 1, 0) + dg(feat, bdw_ref[1], 1, 0) + d_totals
    w = w_ref[...]
    dl = w * (dw - block_sum(w * dw, ones))
    dlt = (dl * inv_temp).astype(bf16)
    big1.step()
    dmid = dg(dlt, bds_ref[...], 1, 1).astype(bf16)
    g3[0:256, :] = dg(normed1t_ref[...], dmid, 1, 0)
    dn = dg(dmid, wmid_ref[...], 1, 1).astype(bf16).astype(f32) + dg(dfeat, wfeat_ref[...], 1, 1).astype(bf16).astype(
        f32
    )
    dn = dn.astype(bf16).astype(f32)
    xhat1, rstd1 = norm_parts(x_ref[...].astype(f32))

    first = (lax.axis_index("point") == 0).astype(f32)
    g3[SMALL:N3, :] = jnp.zeros((N3 - SMALL, 256), f32)
    pick = (iota((HM, 256), 0) // SLICES == iota((HM, 256), 1)).astype(f32)
    inv8 = jnp.zeros((1, 256), f32)
    for h in range(HEADS):
        inv8 = jnp.where(iota((1, 256), 1) == h, 1.0 / temp_ref[h], inv8)
    g_temp = jnp.sum(exact(fold8(dl * l_ref[...]), pick, 1, 0), axis=0, keepdims=True) * (-inv8)
    g3[SMALL : SMALL + 1, :] = jnp.sum(dn * xhat1, axis=0, keepdims=True)
    g3[SMALL + 1 : SMALL + 2, :] = g_gain2
    g3[SMALL + 2 : SMALL + 3, :] = g_temp
    g3[SMALL + 8 : SMALL + 40, 0:64] = exact(gather_heads(dg(midt_ref[...], dlt, 1, 0)), place, 1, 1)
    g3[SMALL + 8 : SMALL + 40, 128:160] = gq * first
    g3[SMALL + 40 : SMALL + 72, 0:32] = gk * first
    g3[SMALL + 40 : SMALL + 72, 128:160] = gv * first
    tail.step()
    mid2.step()
    big1.step()
    cells_ref[...] = (norm_back(dn, xhat1, rstd1, gain1) + dstate_ref[...]).astype(bf16)
    stores[0].start()
    tail.step()
    big1.step()
    mid2.step()
    tail.step()
    big1.step()
    mid2.step()
    tail.step()
    big1.step()
    mid2.step()
    tail.step()
    big1.step()
    stores[1].start()
    mid2.step()
    stores[2].start()
    tail.step()
    stores[3].start()
    for cp in stores:
        cp.wait()


def out_kernel(
    hbm_cells, hbm1, hbm2, hbm3,
    cells_out, gain1, mid, feat, slc, temp, wq, wk, wv, wout, gain2, up, down,
    o1, o3, sems,
):
    part = N1 // 8
    pairs = [(hbm3, o3), (hbm_cells, cells_out), (hbm2.at[0:256, :], wout), (hbm2.at[256:512, :], feat)]
    pairs += [(hbm1.at[k * part : (k + 1) * part, :], o1.at[k * part : (k + 1) * part, :]) for k in range(8)]
    copies = [pltpu.make_async_copy(a, b, sems.at[i]) for i, (a, b) in enumerate(pairs)]
    for cp in copies:
        cp.start()
    copies[0].wait()
    mid[...] = o3[0:256, :]
    gain1[...] = o3[SMALL : SMALL + 1, :]
    gain2[...] = o3[SMALL + 1 : SMALL + 2, :]
    temp[...] = o3[SMALL + 2 : SMALL + 3, 0:8]
    slc[...] = o3[SMALL + 8 : SMALL + 40, 0:64]
    wq[...] = o3[SMALL + 8 : SMALL + 40, 128:160]
    wk[...] = o3[SMALL + 40 : SMALL + 72, 0:32]
    wv[...] = o3[SMALL + 40 : SMALL + 72, 128:160]
    for j in range(4):
        copies[4 + j].wait()
        down[j * 256 : (j + 1) * 256, :] = o1[j * 256 : (j + 1) * 256, :]
    for j in range(4):
        copies[8 + j].wait()
        up[:, j * 256 : (j + 1) * 256] = o1[1024 + j * 256 : 1280 + j * 256, :]
    for cp in copies[1:4]:
        cp.wait()


vmem_ = pl.BlockSpec(memory_space=pltpu.VMEM)
any_ = pl.BlockSpec(memory_space=pl.ANY)


def vmem(count):
    return [vmem_] * count


def anys(count):
    return [any_] * count


def on_device(x, dy, gain1, wmid, wfeat, ws, temp, wq, wk, wv, wout, gain2, wup, wdown):
    sds = jax.ShapeDtypeStruct
    operands = (
        x[0], dy[0], gain1.reshape(1, D), wmid, wfeat, ws, wq, wk, wv, wout, gain2.reshape(1, D), wup, wdown,
    )
    cells, o1, o2, o3 = pl.pallas_call(
        main_kernel,
        out_shape=(sds((CELLS, D), bf16), sds((N1, 256), f32), sds((N2, 256), f32), sds((N3, 256), f32)),
        in_specs=[pl.BlockSpec(memory_space=pltpu.SMEM)] + [pl.BlockSpec(memory_space=pltpu.HBM)] * 13,
        out_specs=[pl.BlockSpec(memory_space=pltpu.HBM)] * 4,
        scratch_shapes=[pltpu.VMEM(a.shape, a.dtype) for a in operands]
        + [
            pltpu.SemaphoreType.DMA((13,)),
            pltpu.VMEM((CELLS, D), bf16),
            pltpu.VMEM((N1, 256), f32),
            pltpu.VMEM((N2, 256), f32),
            pltpu.VMEM((N3, 256), f32),
            pltpu.SemaphoreType.DMA((4,)),
            pltpu.VMEM((CELLS, HM), f32),
            pltpu.VMEM((CELLS, HM), f32),
            pltpu.VMEM((CELLS, FF), bf16),
            pltpu.VMEM((CELLS, FF), bf16),
            pltpu.VMEM((D, CELLS), bf16),
            pltpu.VMEM((D, CELLS), bf16),
            pltpu.VMEM((CELLS, D), f32),
            pltpu.VMEM((CELLS, HM), f32),
            pltpu.VMEM((D, HM), bf16),
            pltpu.VMEM((2, D, HM), bf16),
            pltpu.VMEM((2, D, HM), bf16),
            pltpu.VMEM((4, 128, 128), f32),
        ]
        + small_scratch(24)
        + small_scratch(16)
        + big_scratch(N1)
        + mid_scratch(N2)
        + mid_scratch(N3),
        compiler_params=pltpu.CompilerParams(
            collective_id=0, has_side_effects=True, vmem_limit_bytes=56 * 2**20
        ),
    )(temp, *operands)
    outs = pl.pallas_call(
        out_kernel,
        out_shape=(
            sds((CELLS, D), bf16), sds((1, D), f32), sds((D, D), f32), sds((D, D), f32),
            sds((HEAD_DIM, SLICES), f32), sds((1, HEADS), f32), sds((HEAD_DIM, HEAD_DIM), f32),
            sds((HEAD_DIM, HEAD_DIM), f32), sds((HEAD_DIM, HEAD_DIM), f32), sds((D, D), f32), sds((1, D), f32),
            sds((D, FF), f32), sds((FF, D), f32),
        ),
        in_specs=[pl.BlockSpec(memory_space=pltpu.HBM)] * 4,
        out_specs=vmem(13),
        scratch_shapes=[
            pltpu.VMEM((N1, 256), f32),
            pltpu.VMEM((N3, 256), f32),
            pltpu.SemaphoreType.DMA((12,)),
        ],
        compiler_params=pltpu.CompilerParams(vmem_limit_bytes=56 * 2**20),
    )(cells, o1, o2, o3)
    outs = list(outs)
    outs[0] = outs[0][None]
    outs[1] = outs[1].reshape(D)
    outs[5] = outs[5].reshape(HEADS)
    outs[10] = outs[10].reshape(D)
    return tuple(outs)


def solution(mesh):
    return jax.shard_map(
        on_device,
        mesh=mesh,
        in_specs=(P("dp", "point", None), P("dp", "point", None)) + (P(),) * 12,
        out_specs=(P("dp", "point", None),) + (P(),) * 12,
        check_vma=False,
    )
```

```python
import functools
import jax
import jax.numpy as jnp
from jax import lax
from jax.experimental import pallas as pl
from jax.experimental.pallas import tpu as pltpu
from jax.sharding import PartitionSpec as P

MESH = pl.DeviceIdType.MESH
HIGHEST = lax.Precision.HIGHEST
f32 = jnp.float32
bf16 = jnp.bfloat16

CELLS = 768
D = 256
FF = 1024
HEADS = 8
SLICES = 64
HEAD_DIM = 32
HM = HEADS * SLICES
EPS = 1e-05
N1 = 2048
N2 = 512
N3 = 384
SMALL = 256
GELU_C = 0.7978845608028654
GELU_A = 0.044715


def rcopy(src, dst, ss, rs, dev):
    return pltpu.make_async_remote_copy(
        src_ref=src, dst_ref=dst, send_sem=ss, recv_sem=rs, device_id=dev, device_id_type=MESH
    )


def m8(v):
    return pl.multiple_of(v, 8)


class Place:
    def __init__(self):
        self.y = lax.axis_index("dp")
        p = lax.axis_index("point")
        self.z = p // 8
        self.g = lax.rem(p, 8)
        self.x = self.g // 2
        self.c = lax.rem(self.g, 2)
        z, x, c, g, y = self.z, self.x, self.c, self.g, self.y
        self.core = {"point": z * 8 + x * 2 + (1 - c)}
        self.gp = [{"point": z * 8 + lax.rem(g + d, 8)} for d in range(1, 8)]
        self.zp = [{"point": lax.rem(z + d, 8) * 8 + g} for d in range(1, 8)]
        self.xp = [{"point": z * 8 + lax.rem(x + d, 4) * 2 + c} for d in range(1, 4)]
        self.yp = [{"dp": lax.rem(y + d, 4)} for d in range(1, 4)]
        self.xyp = [
            {"dp": lax.rem(y + d % 4, 4), "point": z * 8 + lax.rem(x + d // 4, 4) * 2 + c} for d in range(1, 16)
        ]
        far = [self.xyp[d - 1] for d in range(1, 16) if d % 4]
        self.everyone = self.gp + self.zp + far


class Stage:
    def __init__(self, ss, rs):
        self.ss, self.rs, self.k, self.pending = ss, rs, -1, None
        self.copies = []

    def wait(self):
        if self.pending is not None:
            self.pending.wait_send()
            self.pending.wait_recv()
        self.pending = None
        self.copies = []

    def begin(self):
        self.wait()
        self.k += 1
        return self.k

    def add(self, src, dst, dev):
        rcopy(src, dst, self.ss.at[self.k], self.rs.at[self.k], dev).start()

    def total(self, ref, dev):
        self.pending = rcopy(ref, ref, self.ss.at[self.k], self.rs.at[self.k], dev)


class SmallSum(Stage):
    def __init__(self, at, s, o, rx1, rx2, ss, rs):
        super().__init__(ss, rs)
        self.at, self.s, self.o, self.rx1, self.rx2 = at, s, o, rx1, rx2

    def step(self):
        at, s, o, rx1, rx2 = self.at, self.s, self.o, self.rx1, self.rx2
        k = self.begin()
        if k == 0:
            for d in range(1, 8):
                self.add(s.at[lax.rem(at.g + d, 8)], rx1.at[d - 1], at.gp[d - 1])
            self.total(rx1, at.gp[0])
        elif k == 1:
            acc = s[at.g]
            for d in range(7):
                acc = acc + rx1[d]
            rx2[at.z] = acc
            mine = rx2.at[at.z]
            for d in range(7):
                self.add(mine, mine, at.zp[d])
            self.total(rx1, at.zp[0])
        elif k == 2:
            acc = rx2[0]
            for d in range(1, 8):
                acc = acc + rx2[d]
            o[at.g] = acc
            mine = o.at[at.g]
            for d in range(7):
                self.add(mine, mine, at.gp[d])
            self.total(rx1, at.gp[0])


def add_rows(dst, d0, base, b0, srcs, rows):
    t = min(rows, 64)

    def body(i, _):
        o = pl.multiple_of(i * t, t)
        acc = base[pl.ds(m8(b0 + o), t), :]
        for s in srcs:
            acc = acc + s[pl.ds(o, t), :]
        dst[pl.ds(m8(d0 + o), t), :] = acc
        return 0

    lax.fori_loop(0, rows // t, body, 0)


class BigSum(Stage):
    def __init__(self, n, at, src, o, bufs, ss, rs):
        super().__init__(ss, rs)
        self.n, self.at, self.src, self.o = n, at, src, o
        self.gref, self.rx0, self.rx1, self.rx2, self.rx3, self.zb, self.zo = bufs
        self.H, self.Q, self.E, self.F = n // 2, n // 4, n // 16, n // 64
        self.K = self.F // 2
        E, F, Q, H = self.E, self.F, self.Q, self.H
        self.h0 = m8(at.c * H)
        self.a0, self.b0 = m8(at.x * E), m8(Q + at.y * E)
        self.a1, self.b1 = m8(self.a0 + at.y * F), m8(self.b0 + at.x * F)

    def zat(self, ref, k):
        K = self.K
        return ref.at[pl.ds(m8((k // 2) * K), K), pl.ds(pl.multiple_of(lax.rem(k, 2) * 128, 128), 128)]

    def step(self):
        at, H, Q, E, F = self.at, self.H, self.Q, self.E, self.F
        gref, rx0, rx1, rx2, rx3, zb, zo, o = (
            self.gref, self.rx0, self.rx1, self.rx2, self.rx3, self.zb, self.zo, self.o,
        )
        h0, a0, b0, a1, b1 = self.h0, self.a0, self.b0, self.a1, self.b1
        k = self.begin()
        if k == 0:
            self.add(self.src.at[pl.ds(m8((1 - at.c) * H), H)], rx0, at.core)
            self.total(rx0, at.core)
        elif k == 1:
            add_rows(gref, 0, self.src, h0, [rx0], H)
            for d in range(1, 4):
                xi, yi = lax.rem(at.x + d, 4), lax.rem(at.y + d, 4)
                self.add(gref.at[pl.ds(m8(xi * E), E)], rx1.at[0, d - 1], at.xp[d - 1])
                self.add(gref.at[pl.ds(m8(Q + yi * E), E)], rx1.at[1, d - 1], at.yp[d - 1])
            self.total(rx1, at.xp[0])
        elif k == 2:
            add_rows(gref, a0, gref, a0, [rx1.at[0, d] for d in range(3)], E)
            add_rows(gref, b0, gref, b0, [rx1.at[1, d] for d in range(3)], E)
            for d in range(1, 4):
                xi, yi = lax.rem(at.x + d, 4), lax.rem(at.y + d, 4)
                self.add(gref.at[pl.ds(m8(a0 + yi * F), F)], rx2.at[0, d - 1], at.yp[d - 1])
                self.add(gref.at[pl.ds(m8(b0 + xi * F), F)], rx2.at[1, d - 1], at.xp[d - 1])
            self.total(rx2, at.xp[0])
        elif k == 3:
            add_rows(zb, 0, gref, a1, [rx2.at[0, d] for d in range(3)], F)
            add_rows(zb, F, gref, b1, [rx2.at[1, d] for d in range(3)], F)
            for d in range(1, 8):
                self.add(self.zat(zb, lax.rem(at.z + d, 8)), rx3.at[d - 1], at.zp[d - 1])
            self.total(rx3, at.zp[0])
        elif k == 4:
            acc = self.zat(zb, at.z)[...]
            for d in range(7):
                acc = acc + rx3[d]
            mine = self.zat(zo, at.z)
            mine[...] = acc
            for d in range(1, 8):
                self.add(mine, mine, at.zp[d - 1])
            self.total(rx3, at.zp[0])
        elif k == 5:
            o[pl.ds(m8(h0 + a1), F), :] = zo[0:F, :]
            o[pl.ds(m8(h0 + b1), F), :] = zo[F : 2 * F, :]
            ra, rb = o.at[pl.ds(m8(h0 + a1), F)], o.at[pl.ds(m8(h0 + b1), F)]
            for d in range(1, 4):
                self.add(ra, ra, at.yp[d - 1])
                self.add(rb, rb, at.xp[d - 1])
            self.total(rx2, at.xp[0])
        elif k == 6:
            ra, rb = o.at[pl.ds(m8(h0 + a0), E)], o.at[pl.ds(m8(h0 + b0), E)]
            for d in range(1, 4):
                self.add(ra, ra, at.xp[d - 1])
                self.add(rb, rb, at.yp[d - 1])
            self.total(rx1, at.xp[0])
        elif k == 7:
            half = o.at[pl.ds(h0, H)]
            self.add(half, half, at.core)
            self.total(rx0, at.core)


class MidSum(Stage):
    def __init__(self, n, at, src, o, bufs, ss, rs):
        super().__init__(ss, rs)
        self.n, self.at, self.src, self.o = n, at, src, o
        self.gref, self.rx0, self.rx1, self.rx2 = bufs
        self.r = n // 16

    def lanes(self, ref, c):
        return ref.at[:, pl.ds(pl.multiple_of(c * 128, 128), 128)]

    def step(self):
        at, r, gref, rx0, rx1, rx2 = self.at, self.r, self.gref, self.rx0, self.rx1, self.rx2
        k = self.begin()
        own = m8((at.x * 4 + at.y) * r)
        if k == 0:
            self.add(self.lanes(self.src, 1 - at.c), rx0, at.core)
            self.total(rx0, at.core)
        elif k == 1:
            gref[...] = self.lanes(self.src, at.c)[...] + rx0[...]
            for d in range(1, 16):
                to = lax.rem(at.x + d // 4, 4) * 4 + lax.rem(at.y + d % 4, 4)
                self.add(gref.at[pl.ds(m8(to * r), r)], rx1.at[d - 1], at.xyp[d - 1])
            self.total(rx1, at.xyp[0])
        elif k == 2:
            acc = gref[pl.ds(own, r), :]
            for d in range(15):
                acc = acc + rx1[d]
            rx2[at.z] = acc
            mine = rx2.at[at.z]
            for d in range(7):
                self.add(mine, mine, at.zp[d])
            self.total(rx2.at[pl.ds(0, 7)], at.zp[0])
        elif k == 3:
            acc = rx2[0]
            for d in range(1, 8):
                acc = acc + rx2[d]
            mine = self.o.at[pl.ds(own, r), pl.ds(pl.multiple_of(at.c * 128, 128), 128)]
            mine[...] = acc
            for d in range(15):
                self.add(mine, mine, at.xyp[d])
            self.total(rx1, at.xyp[0])
        elif k == 4:
            half = self.lanes(self.o, at.c)
            self.add(half, half, at.core)
            self.total(rx0, at.core)


def mid_scratch(n):
    r = n // 16
    return [
        pltpu.VMEM((n, 256), f32),
        pltpu.VMEM((n, 128), f32),
        pltpu.VMEM((n, 128), f32),
        pltpu.VMEM((15, r, 128), f32),
        pltpu.VMEM((8, r, 128), f32),
        pltpu.SemaphoreType.DMA((5,)),
        pltpu.SemaphoreType.DMA((5,)),
    ]


def small_scratch(r):
    return [
        pltpu.VMEM((8, r, 128), f32),
        pltpu.VMEM((8, r, 128), f32),
        pltpu.VMEM((7, r, 128), f32),
        pltpu.VMEM((8, r, 128), f32),
        pltpu.SemaphoreType.DMA((3,)),
        pltpu.SemaphoreType.DMA((3,)),
    ]


def big_scratch(n):
    H, E, F = n // 2, n // 16, n // 64
    return [
        pltpu.VMEM((n, 256), f32),
        pltpu.VMEM((H, 256), f32),
        pltpu.VMEM((H, 256), f32),
        pltpu.VMEM((2, 3, E, 256), f32),
        pltpu.VMEM((2, 3, F, 256), f32),
        pltpu.VMEM((7, F // 2, 128), f32),
        pltpu.VMEM((2 * F, 256), f32),
        pltpu.VMEM((2 * F, 256), f32),
        pltpu.SemaphoreType.DMA((8,)),
        pltpu.SemaphoreType.DMA((8,)),
    ]


def dg(a, b, ca, cb, precision=None):
    return lax.dot_general(a, b, (((ca,), (cb,)), ((), ())), preferred_element_type=f32, precision=precision)


def exact(a, b, ca, cb):
    return dg(a, b, ca, cb, HIGHEST)


def split(v):
    hi = v.astype(bf16)
    return hi, (v - hi.astype(f32)).astype(bf16)


def iota(shape, dim):
    return lax.broadcasted_iota(jnp.int32, shape, dim)


def block_sum(v, ones):
    out = []
    for half in range(2):
        hi, lo = split(v[:, half * 256 : (half + 1) * 256])
        out.append(dg(hi, ones, 1, 0) + dg(lo, ones, 1, 0))
    return jnp.concatenate(out, axis=1)


def spread_heads(t):
    lanes = iota((HEAD_DIM, HM), 1) // SLICES
    return jnp.concatenate([jnp.where(lanes == h, t, 0.0) for h in range(HEADS)], axis=0)


def gather_heads(ref):
    lanes = iota((HEAD_DIM, HM), 1) // SLICES
    acc = jnp.zeros((HEAD_DIM, HM), f32)
    for h in range(HEADS):
        acc = jnp.where(lanes == h, ref[h * HEAD_DIM : (h + 1) * HEAD_DIM, :], acc)
    return acc


def mean_rows(v):
    return jnp.sum(v, axis=1, keepdims=True) * (1.0 / D)


def norm_parts(v):
    centred = v - mean_rows(v)
    rstd = lax.rsqrt(mean_rows(centred * centred) + EPS)
    return centred * rstd, rstd


def norm_back(dn, xhat, rstd, gain):
    dxh = dn * gain
    return rstd * (dxh - mean_rows(dxh) - xhat * mean_rows(dxh * xhat))


def fold8(v):
    return jnp.sum(v.reshape(v.shape[0] // 8, 8, v.shape[1]), axis=0)


def main_kernel(
    temp_ref, *rest,
):
    hbm, outs, bufs, load_sem, rest = rest[:13], rest[13:17], rest[17:30], rest[30], rest[31:]
    results, store_sem, rest = rest[:4], rest[4], rest[5:]
    x_ref, dy_ref, gain1_ref, wmid_ref, wfeat_ref, ws_ref, wq_ref, wk_ref, wv_ref, wout_ref, gain2_ref, wup_ref, wdown_ref = bufs
    (
    cells_ref, o1_ref, o2_ref, o3_ref,
    ) = results
    stores = [pltpu.make_async_copy(results[i], outs[i], store_sem.at[i]) for i in range(4)]
    (
    l_ref, w_ref, du_ref, dh_ref, normed1t_ref, midt_ref, dstate_ref, dw2_ref, bds_ref, bdm_ref, bdw_ref, p_ref,
    s1, so1, s1a, s1b, ss1, rs1, s2, so2, s2a, s2b, ss2, rs2,
    g1, g1a, g1b, g1c, g1d, g1e, g1f, g1g, ss3, rs3, g2, g2a, g2b, g2c, g2d, ss4, rs4,
    g3, g3a, g3b, g3c, g3d, ss5, rs5,
    ) = rest
    loads = [pltpu.make_async_copy(hbm[i], bufs[i], load_sem.at[i]) for i in range(13)]
    for i in (0, 3, 4, 2, 5, 6, 7, 8, 9, 10, 1, 11, 12):
        loads[i].start()
    at = Place()
    everyone = at.everyone
    sem = pltpu.get_barrier_semaphore()
    for dev in everyone:
        pl.semaphore_signal(sem, inc=1, device_id=dev, device_id_type=MESH)
    sum1 = SmallSum(at, s1, so1, s1a, s1b, ss1, rs1)
    sum2 = SmallSum(at, s2, so2, s2a, s2b, ss2, rs2)
    big1 = BigSum(N1, at, g1, o1_ref, (g1a, g1b, g1c, g1d, g1e, g1f, g1g), ss3, rs3)
    mid2 = MidSum(N2, at, g2, o2_ref, (g2a, g2b, g2c, g2d), ss4, rs4)
    tail = MidSum(N3, at, g3, o3_ref, (g3a, g3b, g3c, g3d), ss5, rs5)

    for i in (0, 3, 4, 2, 5):
        loads[i].wait()

    head_of_lane = iota((1, HM), 1) // SLICES
    temp = jnp.zeros((1, HM), f32)
    for h in range(HEADS):
        temp = jnp.where(head_of_lane == h, temp_ref[h], temp)
    inv_temp = 1.0 / temp
    ones = (iota((256, 256), 0) // SLICES == iota((256, 256), 1) // SLICES).astype(f32).astype(bf16)
    place = (iota((SLICES, HM), 0) == lax.rem(iota((SLICES, HM), 1), SLICES)).astype(f32)
    wide = dg(ws_ref[...], place.astype(bf16), 1, 0)
    bds_ref[...] = spread_heads(wide).astype(bf16)
    gain1 = gain1_ref[...]

    xhat1, rstd1 = norm_parts(x_ref[...].astype(f32))
    normed1 = (xhat1 * gain1).astype(bf16)
    mid = dg(normed1, wmid_ref[...], 1, 0)
    feat = dg(normed1, wfeat_ref[...], 1, 0).astype(bf16)
    mid_hi, mid_lo = split(mid)
    logits = (dg(mid_hi, bds_ref[...], 1, 0) + dg(mid_lo, bds_ref[...], 1, 0)) * inv_temp
    l_ref[...] = logits
    e = jnp.exp(logits)
    w = e / block_sum(e, ones)
    w_ref[...] = w
    wb = w.astype(bf16)
    tt = gather_heads(dg(feat, wb, 0, 0))
    tot = fold8(w)
    for j in range(8):
        lanes = slice((j // 2) * 128, (j // 2 + 1) * 128)
        s1[j, 0:16, :] = tt[(j % 2) * 16 : (j % 2 + 1) * 16, lanes]
        s1[j, 16:24, :] = tot[:, lanes]

    pl.semaphore_wait(sem, len(everyone))
    sum1.step()
    for i in (1, 12):
        loads[i].wait()
    dy = dy_ref[...]
    for j in range(2):
        cols = slice(j * 256, (j + 1) * 256)
        dh_ref[:, cols] = dg(dy, wdown_ref[cols, :], 1, 1).astype(bf16)
    sum1.step()
    for j in range(2, 4):
        cols = slice(j * 256, (j + 1) * 256)
        dh_ref[:, cols] = dg(dy, wdown_ref[cols, :], 1, 1).astype(bf16)
    sum1.step()
    normed1t_ref[...] = normed1.T
    midt_ref[...] = mid_hi.T
    for i in (6, 7, 8, 9, 10, 11):
        loads[i].wait()
    gain2 = gain2_ref[...]
    sum1.wait()

    wq, wk, wv = (r[...].astype(f32) for r in (wq_ref, wk_ref, wv_ref))
    scale = HEAD_DIM**-0.5
    same = iota((128, 128), 0) // SLICES == iota((128, 128), 1) // SLICES
    mix = []
    kept = []
    for b in range(4):
        total = jnp.sum(so1[2 * b, 16:24, :], axis=0, keepdims=True)
        tok = jnp.concatenate([so1[2 * b, 0:16, :], so1[2 * b + 1, 0:16, :]], axis=0) / total
        q = exact(wq, tok, 0, 0)
        k = exact(wk, tok, 0, 0)
        v = exact(wv, tok, 0, 0)
        sc = exact(q, k, 0, 0) * scale
        e = jnp.where(same, jnp.exp(jnp.where(same, sc, 0.0)), 0.0)
        prob = e / jnp.sum(e, axis=1, keepdims=True)
        p_ref[b] = prob
        mix.append(exact(v, prob, 1, 1))
        kept.append((total, tok, q, k, v))
    hi, lo = split(spread_heads(jnp.concatenate(mix, axis=1)))
    bdm_ref[0] = hi
    bdm_ref[1] = lo

    sp = dg(wb, bdm_ref[0], 1, 1).astype(bf16)
    state = x_ref[...].astype(f32) + dg(sp, wout_ref[...], 1, 0)
    xhat2, rstd2 = norm_parts(state)
    normed2 = (xhat2 * gain2).astype(bf16)
    normed2t = normed2.T
    dy = dy_ref[...]
    for j in range(4):
        cols = slice(j * 256, (j + 1) * 256)
        u = dg(normed2, wup_ref[:, cols], 1, 0)
        u2 = u * u
        t = jnp.tanh(u * (GELU_C + (GELU_C * GELU_A) * u2))
        half = 0.5 + 0.5 * t
        hidden = (u * half).astype(bf16)
        slope = half + u * half * (1.0 - t) * (GELU_C + (3.0 * GELU_C * GELU_A) * u2)
        du = (dh_ref[:, cols].astype(f32) * slope).astype(bf16)
        du_ref[:, cols] = du
        g1[j * 256 : (j + 1) * 256, :] = dg(hidden, dy, 0, 0)
        g1[1024 + j * 256 : 1280 + j * 256, :] = dg(normed2t, du, 1, 0)
    dn = dg(du_ref[...], wup_ref[...], 1, 1).astype(bf16).astype(f32)
    g_gain2 = jnp.sum(dn * xhat2, axis=0, keepdims=True)
    ds = dy.astype(f32) + norm_back(dn, xhat2, rstd2, gain2)
    dstate_ref[...] = ds
    dsb = ds.astype(bf16)
    dsp = dg(dsb, wout_ref[...], 1, 1).astype(bf16)
    dmt = gather_heads(dg(dsp, wb, 0, 0))
    for j in range(8):
        s2[j] = dmt[(j % 2) * 16 : (j % 2 + 1) * 16, (j // 2) * 128 : (j // 2 + 1) * 128]
    sum2.step()
    big1.step()
    dw2_ref[...] = dg(dsp, bdm_ref[0], 1, 0) + dg(dsp, bdm_ref[1], 1, 0)
    sum2.step()
    big1.step()
    g2[0:256, :] = dg(sp, dsb, 0, 0)
    sum2.step()
    sum2.wait()

    big1.step()
    gq = jnp.zeros((HEAD_DIM, HEAD_DIM), f32)
    gk, gv = gq, gq
    dwt, dtot = [], []
    for b in range(4):
        total, tok, q, k, v = kept[b]
        prob = p_ref[b]
        dm = jnp.concatenate([so2[2 * b], so2[2 * b + 1]], axis=0)
        dp = exact(dm, v, 0, 0)
        dsc = prob * (dp - jnp.sum(prob * dp, axis=1, keepdims=True)) * scale
        dq = exact(k, dsc, 1, 1)
        dk = exact(q, dsc, 1, 0)
        dv = exact(dm, prob, 1, 0)
        gq = gq + exact(tok, dq, 1, 1)
        gk = gk + exact(tok, dk, 1, 1)
        gv = gv + exact(tok, dv, 1, 1)
        dtok = exact(wq, dq, 1, 0) + exact(wk, dk, 1, 0) + exact(wv, dv, 1, 0)
        dtok = dtok / total
        dwt.append(dtok)
        dtot.append(-jnp.sum(dtok * tok, axis=0, keepdims=True))
    hi, lo = split(spread_heads(jnp.concatenate(dwt, axis=1)))
    bdw_ref[0] = hi
    bdw_ref[1] = lo
    d_totals = jnp.concatenate(dtot, axis=1)

    dfeat = dg(wb, bdw_ref[0], 1, 1).astype(bf16)
    g2[256:512, :] = dg(normed1t_ref[...], dfeat, 1, 0)
    mid2.step()
    dw = dw2_ref[...] + dg(feat, bdw_ref[0], 1, 0) + dg(feat, bdw_ref[1], 1, 0) + d_totals
    w = w_ref[...]
    dl = w * (dw - block_sum(w * dw, ones))
    dlt = (dl * inv_temp).astype(bf16)
    big1.step()
    dmid = dg(dlt, bds_ref[...], 1, 1).astype(bf16)
    g3[0:256, :] = dg(normed1t_ref[...], dmid, 1, 0)
    dn = dg(dmid, wmid_ref[...], 1, 1).astype(bf16).astype(f32) + dg(dfeat, wfeat_ref[...], 1, 1).astype(bf16).astype(
        f32
    )
    dn = dn.astype(bf16).astype(f32)
    xhat1, rstd1 = norm_parts(x_ref[...].astype(f32))

    first = (lax.axis_index("point") == 0).astype(f32)
    g3[SMALL:N3, :] = jnp.zeros((N3 - SMALL, 256), f32)
    pick = (iota((HM, 256), 0) // SLICES == iota((HM, 256), 1)).astype(f32)
    inv8 = jnp.zeros((1, 256), f32)
    for h in range(HEADS):
        inv8 = jnp.where(iota((1, 256), 1) == h, 1.0 / temp_ref[h], inv8)
    g_temp = jnp.sum(exact(fold8(dl * l_ref[...]), pick, 1, 0), axis=0, keepdims=True) * (-inv8)
    g3[SMALL : SMALL + 1, :] = jnp.sum(dn * xhat1, axis=0, keepdims=True)
    g3[SMALL + 1 : SMALL + 2, :] = g_gain2
    g3[SMALL + 2 : SMALL + 3, :] = g_temp
    g3[SMALL + 8 : SMALL + 40, 0:64] = exact(gather_heads(dg(midt_ref[...], dlt, 1, 0)), place, 1, 1)
    g3[SMALL + 8 : SMALL + 40, 128:160] = gq * first
    g3[SMALL + 40 : SMALL + 72, 0:32] = gk * first
    g3[SMALL + 40 : SMALL + 72, 128:160] = gv * first
    tail.step()
    mid2.step()
    big1.step()
    tail.step()
    cells_ref[...] = (norm_back(dn, xhat1, rstd1, gain1) + dstate_ref[...]).astype(bf16)
    stores[0].start()
    big1.step()
    mid2.step()
    tail.step()
    big1.step()
    mid2.step()
    tail.step()
    big1.step()
    mid2.step()
    tail.step()
    big1.step()
    stores[1].start()
    mid2.step()
    stores[2].start()
    tail.step()
    stores[3].start()
    for cp in stores:
        cp.wait()


def out_kernel(
    hbm_cells, hbm1, hbm2, hbm3,
    cells_out, gain1, mid, feat, slc, temp, wq, wk, wv, wout, gain2, up, down,
    o1, o3, sems,
):
    part = N1 // 8
    pairs = [(hbm3, o3), (hbm_cells, cells_out), (hbm2.at[0:256, :], wout), (hbm2.at[256:512, :], feat)]
    pairs += [(hbm1.at[k * part : (k + 1) * part, :], o1.at[k * part : (k + 1) * part, :]) for k in range(8)]
    copies = [pltpu.make_async_copy(a, b, sems.at[i]) for i, (a, b) in enumerate(pairs)]
    for cp in copies:
        cp.start()
    copies[0].wait()
    mid[...] = o3[0:256, :]
    gain1[...] = o3[SMALL : SMALL + 1, :]
    gain2[...] = o3[SMALL + 1 : SMALL + 2, :]
    temp[...] = o3[SMALL + 2 : SMALL + 3, 0:8]
    slc[...] = o3[SMALL + 8 : SMALL + 40, 0:64]
    wq[...] = o3[SMALL + 8 : SMALL + 40, 128:160]
    wk[...] = o3[SMALL + 40 : SMALL + 72, 0:32]
    wv[...] = o3[SMALL + 40 : SMALL + 72, 128:160]
    for j in range(4):
        copies[4 + j].wait()
        down[j * 256 : (j + 1) * 256, :] = o1[j * 256 : (j + 1) * 256, :]
    for j in range(4):
        copies[8 + j].wait()
        up[:, j * 256 : (j + 1) * 256] = o1[1024 + j * 256 : 1280 + j * 256, :]
    for cp in copies[1:4]:
        cp.wait()


vmem_ = pl.BlockSpec(memory_space=pltpu.VMEM)
any_ = pl.BlockSpec(memory_space=pl.ANY)


def vmem(count):
    return [vmem_] * count


def anys(count):
    return [any_] * count


def on_device(x, dy, gain1, wmid, wfeat, ws, temp, wq, wk, wv, wout, gain2, wup, wdown):
    sds = jax.ShapeDtypeStruct
    operands = (
        x[0], dy[0], gain1.reshape(1, D), wmid, wfeat, ws, wq, wk, wv, wout, gain2.reshape(1, D), wup, wdown,
    )
    cells, o1, o2, o3 = pl.pallas_call(
        main_kernel,
        out_shape=(sds((CELLS, D), bf16), sds((N1, 256), f32), sds((N2, 256), f32), sds((N3, 256), f32)),
        in_specs=[pl.BlockSpec(memory_space=pltpu.SMEM)] + [pl.BlockSpec(memory_space=pltpu.HBM)] * 13,
        out_specs=[pl.BlockSpec(memory_space=pltpu.HBM)] * 4,
        scratch_shapes=[pltpu.VMEM(a.shape, a.dtype) for a in operands]
        + [
            pltpu.SemaphoreType.DMA((13,)),
            pltpu.VMEM((CELLS, D), bf16),
            pltpu.VMEM((N1, 256), f32),
            pltpu.VMEM((N2, 256), f32),
            pltpu.VMEM((N3, 256), f32),
            pltpu.SemaphoreType.DMA((4,)),
            pltpu.VMEM((CELLS, HM), f32),
            pltpu.VMEM((CELLS, HM), f32),
            pltpu.VMEM((CELLS, FF), bf16),
            pltpu.VMEM((CELLS, FF), bf16),
            pltpu.VMEM((D, CELLS), bf16),
            pltpu.VMEM((D, CELLS), bf16),
            pltpu.VMEM((CELLS, D), f32),
            pltpu.VMEM((CELLS, HM), f32),
            pltpu.VMEM((D, HM), bf16),
            pltpu.VMEM((2, D, HM), bf16),
            pltpu.VMEM((2, D, HM), bf16),
            pltpu.VMEM((4, 128, 128), f32),
        ]
        + small_scratch(24)
        + small_scratch(16)
        + big_scratch(N1)
        + mid_scratch(N2)
        + mid_scratch(N3),
        compiler_params=pltpu.CompilerParams(
            collective_id=0, has_side_effects=True, vmem_limit_bytes=56 * 2**20
        ),
    )(temp, *operands)
    outs = pl.pallas_call(
        out_kernel,
        out_shape=(
            sds((CELLS, D), bf16), sds((1, D), f32), sds((D, D), f32), sds((D, D), f32),
            sds((HEAD_DIM, SLICES), f32), sds((1, HEADS), f32), sds((HEAD_DIM, HEAD_DIM), f32),
            sds((HEAD_DIM, HEAD_DIM), f32), sds((HEAD_DIM, HEAD_DIM), f32), sds((D, D), f32), sds((1, D), f32),
            sds((D, FF), f32), sds((FF, D), f32),
        ),
        in_specs=[pl.BlockSpec(memory_space=pltpu.HBM)] * 4,
        out_specs=vmem(13),
        scratch_shapes=[
            pltpu.VMEM((N1, 256), f32),
            pltpu.VMEM((N3, 256), f32),
            pltpu.SemaphoreType.DMA((12,)),
        ],
        compiler_params=pltpu.CompilerParams(vmem_limit_bytes=56 * 2**20),
    )(cells, o1, o2, o3)
    outs = list(outs)
    outs[0] = outs[0][None]
    outs[1] = outs[1].reshape(D)
    outs[5] = outs[5].reshape(HEADS)
    outs[10] = outs[10].reshape(D)
    return tuple(outs)


def solution(mesh):
    return jax.shard_map(
        on_device,
        mesh=mesh,
        in_specs=(P("dp", "point", None), P("dp", "point", None)) + (P(),) * 12,
        out_specs=(P("dp", "point", None),) + (P(),) * 12,
        check_vma=False,
    )
```
